128 devices in a mesh: ctx: 32 (over z_hi, y, x), tp: 4 (over z_lo, core).
Axes of the slice: x: 4, y: 4, z: 4 (z_hi: 2, z_lo: 2; z = z_hi * 2 + z_lo), core: 2. Of those that a mesh axis runs over, the one named last changes fastest.
Arguments:
- tokens: bfloat16 [49152, 4096], P(('ctx', 'tp')), may hold values from -8 to 8
- norm_gain: bfloat16 [4096], replicated, may hold values from 0.25 to 1.75
- w_in: bfloat16 [4096, 3, 2048], P(None, None, 'tp'), may hold values from -0.09375 to 0.09375
- short_weight: bfloat16 [7, 3, 2048], P(None, None, 'tp'), may hold values from -2 to 2
- conv_bias: float32 [2048], P('tp'), may hold values from -4 to 4
- decay_rates: float32 [16, 2048], P(None, 'tp'), may hold values from 0 to 1, as said below
- residues: float32 [16, 2048], P(None, 'tp'), may hold values from -1.5 to 1.5
- w_out: bfloat16 [2048, 4096], P('tp'), may hold values from -0.125 to 0.125
Outputs:
- mixed: bfloat16 [49152, 4096], P(('ctx', 'tp'))
The draws below stay inside these ranges and needn't reach their ends.
Inputs may be any that keep to these rules, and one draw needn't show every extreme that they name: `decay_rates`: every rate lies between 1 / 98304 and 1/30.
All inputs are finite; a program needn't handle non-finite values.
Results may differ from the reference program's by a relative error of at most 0.015.
Values may be sent and summed in bfloat16 or wider, within the bound.
A program may use at most 192 MiB of HBM per device.

```python
import math
import jax
import jax.numpy as jnp
from jax import lax

D = 4096
HC = 2048
K = 7
MODES = 16
SEQ = 49152
N_TP = 4


def draw_tokens(key, part):
    key = jax.random.fold_in(key, 11)
    key_noise, key_rows, key_cols = jax.random.split(key, 3)
    row_scale = jnp.exp(jax.random.uniform(key_rows, (SEQ, 1), jnp.float32, math.log(0.3), math.log(3.0)))
    col_scale = jnp.exp(jax.random.uniform(key_cols, (1, D), jnp.float32, math.log(0.5), math.log(2.0)))
    noise = jnp.clip(jax.random.normal(key_noise, (SEQ, D), jnp.float32), -6.0, 6.0)
    return jnp.clip(noise * row_scale * col_scale, -8.0, 8.0).astype(jnp.bfloat16)


def draw_decay_rates(key, part):
    key = jax.random.fold_in(key, 23)
    key_spread = jax.random.fold_in(key, 0)
    fastest = math.log(1.0 / 30.0)
    slowest = math.log(1.0 / (2.0 * SEQ))
    spread = jax.random.uniform(key_spread, (MODES, HC), jnp.float32, slowest, fastest)
    return jnp.exp(spread).astype(jnp.float32)


def level_of(rng, dims, cuts, smallest, top_value):
    factor_of = 1.0
    for axis_at, shards_of in cuts:
        heights = jax.random.uniform(jax.random.fold_in(jax.random.fold_in(rng, 6), axis_at), (shards_of,), jnp.float32, smallest / len(cuts), top_value / len(cuts))
        factor_of = factor_of * jnp.repeat(jnp.exp(heights), dims[axis_at] // shards_of).reshape((-1,) + (1,) * (len(dims) - 1 - axis_at))
    return factor_of


def scatter_about(own_key, shape, deviation, bound, pieces=(), kind=jnp.bfloat16):
    drawn = jax.random.normal(own_key, shape, jnp.float32) * deviation
    if len(pieces) > 0:
        drawn = level_of(own_key, shape, pieces, -0.22, 0.18) * drawn
    return jnp.clip(drawn, min=-bound, max=bound).astype(kind)


def setup_inputs(seed: int = 0) -> dict:
    arg_keys = jax.random.split(jax.random.key(seed), 9)
    return {
        "tokens": draw_tokens(jax.random.fold_in(arg_keys[8], 71), 0),
        "norm_gain": jnp.clip(1.0 + 0.15 * jax.random.normal(arg_keys[1], (D,), jnp.float32), 0.25, 1.75).astype(jnp.bfloat16),
        "w_in": scatter_about(arg_keys[2], (D, 3, HC), D ** -0.5, 0.09375, ((2, 4),)),
        "short_weight": scatter_about(arg_keys[3], (K, 3, HC), K ** -0.5, 2.0, ((2, 4),)),
        "conv_bias": scatter_about(arg_keys[4], (HC,), 1.0, 4.0, ((0, 4),), jnp.float32),
        "decay_rates": draw_decay_rates(jax.random.fold_in(arg_keys[8], 71), 0),
        "residues": scatter_about(arg_keys[6], (MODES, HC), MODES ** -0.5, 1.5, ((1, 4),), jnp.float32),
        "w_out": scatter_about(arg_keys[7], (HC, D), HC ** -0.5, 0.125, ((0, 4),)),
    }


def short_filter(streams, tap_weights):
    tap_count = tap_weights.shape[0]
    length = streams.shape[0]
    padded = jnp.pad(streams, ((tap_count - 1, 0), (0, 0), (0, 0)))
    summed = jnp.zeros_like(streams)
    for tap_index in range(tap_count):
        offset = tap_count - 1 - tap_index
        summed = summed + tap_weights[tap_index].astype(jnp.float32) * padded[offset:offset + length]
    return summed

def long_filter(product, decay_rates, residues, conv_bias):
    length = product.shape[0]
    channels = product.shape[1]
    blocks = channels // 16
    signal = product.astype(jnp.float32).T.reshape(blocks, 16, length)
    decays = decay_rates.T.reshape(blocks, 16, -1)
    scales = (residues * jnp.sqrt(2.0 * decay_rates)).T.reshape(blocks, 16, -1)
    time_axis = jnp.arange(length, dtype=jnp.float32)

    def one_block(inputs):
        values, block_decays, block_scales = inputs
        kernel = lax.optimization_barrier(jnp.sum(block_scales[:, :, None] * jnp.exp(-block_decays[:, :, None] * time_axis[None, None, :]), axis=1))
        fft_size = 2 * length
        spectrum = jnp.fft.rfft(values, fft_size) * jnp.fft.rfft(kernel, fft_size)
        return jnp.fft.irfft(spectrum, fft_size)[:, :length]
    result = lax.map(one_block, (signal, decays, scales)).reshape(channels, length).T
    return result + conv_bias[None, :] * product.astype(jnp.float32)

def reference(tokens, norm_gain, w_in, short_weight, conv_bias, decay_rates, residues, w_out):
    widened = tokens.astype(jnp.float32)
    normed = (widened * lax.rsqrt(lax.optimization_barrier(jnp.mean(widened * widened, axis=1, keepdims=True)) + 1e-06) * norm_gain.astype(jnp.float32)).astype(jnp.bfloat16)
    projected = jnp.dot(normed, w_in.reshape(D, 3 * HC), preferred_element_type=jnp.float32).astype(jnp.bfloat16)
    filtered = short_filter(projected.reshape(SEQ, 3, HC).astype(jnp.float32), short_weight)
    product = (filtered[:, 1] * filtered[:, 2]).astype(jnp.bfloat16)
    convolved = long_filter(product, decay_rates, residues, conv_bias).astype(jnp.bfloat16)
    convolved = lax.optimization_barrier(convolved)
    gated_rows = (filtered[:, 0] * convolved.astype(jnp.float32)).astype(jnp.bfloat16)
    channel_span = HC // N_TP
    summed = widened
    for block_index in range(N_TP):
        low = block_index * channel_span
        partial_value = jnp.dot(gated_rows[:, low:low + channel_span], w_out[low:low + channel_span], preferred_element_type=jnp.float32).astype(jnp.bfloat16)
        partial_value = lax.optimization_barrier(partial_value)
        summed = summed + partial_value.astype(jnp.float32)
    return summed.astype(jnp.bfloat16)
```

```python
import functools

import jax
import jax.numpy as jnp
from jax import lax
from jax.experimental import pallas as pl
from jax.experimental.pallas import tpu as pltpu
from jax.sharding import PartitionSpec as P

MESH = pl.DeviceIdType.MESH
BF, F32 = jnp.bfloat16, jnp.float32

ROWS = 384
HALO = 16
SLOT = ROWS + HALO
WIDTH = 4096
CH = 512
CHUNKS = 5
CROWS = SLOT // CHUNKS
ORDER = (1, 0, 2, 3, 4)
PIECES = 8
STEPS = ROWS // PIECES
MODES = 16
TAPS = 7
LG = CH // 128
STATE = F32
UNROLL = 6

S_HALO = 0
S_XZ = 1
S_XD = S_XZ + CHUNKS
S_XF = S_XD + CHUNKS
S_WZ = S_XF + CHUNKS
S_WD = S_WZ + 2
S_WA = S_WD + 1
S_WB = S_WA + 6
S_WC = S_WB + 6
S_E1 = S_WC + 1
S_E2 = S_E1 + 7
S_G = S_E2 + 3
S_N = S_G + 3
L_TOK = 0
L_WIN = CHUNKS
L_WO = L_WIN + 3
L_RES = L_WO + 1
L_OUT = L_RES + 1
OUT_TILES = 8
L_N = L_OUT + OUT_TILES
OUT_COLS = WIDTH // OUT_TILES


def kernel(
    tok, gain, w3, taps, bias, decay, resid, w_out, out,
    xo, xr, wi, wo, proj, gs, gg, tapb, ab, wb, lb, bb, lam, xe, et, sin, r1, r2, ss, rs, ls,
):
    ctx = lax.axis_index("ctx")
    tp = lax.axis_index("tp")
    x = lax.rem(ctx, 4)
    y = lax.rem(lax.div(ctx, 4), 4)
    h = lax.div(ctx, 16)
    p = lax.div(tp, 2)
    k = lax.rem(tp, 2)
    z = 2 * h + p
    s = 2 * k - 1

    def dev(dx, dy, dz, core):
        zz = lax.rem(dz + 4, 4)
        return (lax.div(zz, 2) * 16 + lax.rem(dy, 4) * 4 + lax.rem(dx, 4), lax.rem(zz, 2) * 2 + core)

    order_at = ctx * 4 + tp
    nxt = lax.rem(order_at + 1, 128)
    prv = lax.rem(order_at + 127, 128)
    nxt = (lax.div(nxt, 4), lax.rem(nxt, 4))
    prv = (lax.div(prv, 4), lax.rem(prv, 4))
    other = dev(x, y, z, 1 - k)
    partner = dev(x, y, z + s, 1 - k)
    gate_to = dev(x, y, z - s, k)
    gate_from = dev(x, y, z + s, k)
    x_peers = [dev(x + d, y, z, k) for d in (1, 2, 3)]
    y_peers = [dev(x, y + d, z, k) for d in (1, 2, 3)]
    line_at = h * 4 + x
    line_peers = []
    for d in range(1, 8):
        at = lax.rem(line_at + d, 8)
        line_peers.append((lax.div(at, 4) * 16 + y * 4 + lax.rem(at, 4), tp))
    own_j = 2 * p + k
    oth_j = 2 * p + 1 - k
    far_j = 2 * (1 - p) + 1 - k
    far2_j = 2 * (1 - p) + k

    def remote(src, dst, at, to):
        return pltpu.make_async_remote_copy(
            src_ref=src, dst_ref=dst, send_sem=ss.at[at], recv_sem=rs.at[at], device_id=to, device_id_type=MESH
        )

    def local(src, dst, at):
        return pltpu.make_async_copy(src, dst, ls.at[at])

    tok_copies = {}
    for c in ORDER:
        first = 0 if c == 0 else c * CROWS - HALO
        count = CROWS - HALO if c == 0 else CROWS
        tok_copies[c] = local(tok.at[pl.ds(first, count)], xo.at[k, pl.ds(first + HALO, count)], L_TOK + c)
        tok_copies[c].start()
    win_copies = [local(w3.at[i], wi.at[i], L_WIN + i) for i in range(3)]
    for cp in win_copies:
        cp.start()
    wo_copy = local(w_out, wo.at[own_j], L_WO)
    wo_copy.start()

    barrier = pltpu.get_barrier_semaphore()
    greet = [nxt, prv, other, partner, gate_to, gate_from] + y_peers + line_peers
    for to in greet:
        pl.semaphore_signal(barrier, inc=1, device_id=to, device_id_type=MESH)
    pl.semaphore_wait(barrier, len(greet))

    halo_copy = remote(tok.at[pl.ds(ROWS - HALO, HALO)], xo.at[1 - k, pl.ds(0, HALO)], S_HALO, nxt)
    halo_copy.start()
    row_a = pl.multiple_of((y * 4 + x) * 16, 16)
    row_b = pl.multiple_of(256 + (x * 4 + y) * 16, 16)
    wz = [
        remote(w_out.at[pl.ds(r, 16)], wo.at[own_j, pl.ds(r, 16)], S_WZ + i, partner)
        for i, r in enumerate((row_a, row_b))
    ]
    for cp in wz:
        cp.start()

    def norm_rows(first, count):
        def body(i, _):
            at = pl.ds(pl.multiple_of(first + i * 16, 16), 16)
            v = xo[k, at, :].astype(F32)
            scale = lax.rsqrt(jnp.mean(v * v, axis=1, keepdims=True) + 1e-6)
            xo[k, at, :] = (v * scale * gain[...].astype(F32)).astype(BF)
            return 0

        lax.fori_loop(0, count // 16, body, 0)

    xz, xd, xf = {}, {}, {}
    for c in ORDER:
        tok_copies[c].wait()
        if c == 0:
            halo_copy.wait_recv()

            @pl.when(order_at == 0)
            def _():
                xo[k, pl.ds(0, HALO), :] = jnp.zeros((HALO, WIDTH), BF)

        norm_rows(c * CROWS, CROWS)
        part = xo.at[k, pl.ds(c * CROWS, CROWS)]
        xz[c] = remote(part, xr.at[c, 1 - k], S_XZ + c, partner)
        xz[c].start()
        xd[c] = remote(part, part, S_XD + c, other)
        xd[c].start()
        xf[c] = remote(xr.at[c, k], xr.at[c, k], S_XF + c, other)

    for cp in wz:
        cp.wait_recv()
    wa, wbig = [], []
    for i in range(3):
        wa.append(remote(wo.at[far_j, pl.ds(row_a, 16)], wo.at[far_j, pl.ds(row_a, 16)], S_WA + i, x_peers[i]))
        wa.append(remote(wo.at[far_j, pl.ds(row_b, 16)], wo.at[far_j, pl.ds(row_b, 16)], S_WA + 3 + i, y_peers[i]))
    for cp in wa:
        cp.start()

    rate = decay[...]
    weight = resid[...] * jnp.sqrt(2.0 * rate)
    fall = jnp.exp(-rate)
    tap_rows = taps[...].astype(F32)
    for g in range(LG):
        cols = slice(g * 128, (g + 1) * 128)
        lam[g] = rate[:, cols]
        bb[g] = jnp.broadcast_to(bias[:, cols], (8, 128))
        for r in range(MODES):
            lb[g, r] = jnp.broadcast_to(rate[r : r + 1, cols], (8, 128))
            ab[g, r] = jnp.broadcast_to(fall[r : r + 1, cols], (8, 128))
            wb[g, r] = jnp.broadcast_to(weight[r : r + 1, cols], (8, 128))
        for j in range(TAPS):
            for i in range(3):
                tapb[g, j, i] = jnp.broadcast_to(tap_rows[i, j : j + 1, cols], (8, 128))

    def project_own(slot):
        def body(n, _):
            i = lax.div(n, 2)
            cols = pl.ds(pl.multiple_of(lax.rem(n, 2) * 256, 256), 256)
            v = jnp.dot(xo[slot], wi[i, :, cols], preferred_element_type=F32)
            proj[slot * 12 + 2 * n] = v[:, :128]
            proj[slot * 12 + 2 * n + 1] = v[:, 128:]
            return 0

        lax.fori_loop(0, 6, body, 0)

    def project_far(c):
        rows = pl.ds(c * CROWS, CROWS)

        def body(n, _):
            i = lax.div(n, 2)
            cols = pl.ds(pl.multiple_of(lax.rem(n, 2) * 256, 256), 256)
            lhs = xr[c].reshape(2 * CROWS, WIDTH)
            v = jnp.dot(lhs, wi[i, :, cols], preferred_element_type=F32)
            for a in range(2):
                for b in range(2):
                    proj[(2 + a) * 12 + 2 * n + b, rows] = v[a * CROWS : (a + 1) * CROWS, b * 128 : (b + 1) * 128]
            return 0

        lax.fori_loop(0, 6, body, 0)

    def spread(i):
        return pl.ds(HALO + i, PIECES, stride=STEPS)

    def fir(slot, g):
        base = slot * 12 + g
        weights = [tapb[g, j] for j in range(TAPS)]

        def row(at):
            return jnp.stack([proj[base + 4 * i, at, :] for i in range(3)])

        def body(n, past):
            past = list(past)
            for u in range(UNROLL):
                at = spread(n * UNROLL + u)
                now = row(at)
                total = weights[0] * now
                for j in range(1, TAPS):
                    total = total + weights[j] * past[-j]
                past = past[1:] + [now]
                proj[base, at, :] = total[0]
                proj[base + 4, at, :] = total[1] * total[2]
            return tuple(past)

        past = tuple(row(spread(m - (TAPS - 1))) for m in range(TAPS - 1))
        lax.fori_loop(0, STEPS // UNROLL, body, past)

    lane8 = lax.broadcasted_iota(jnp.int32, (1, 8, 128), 1)

    def scan(slot, g):
        base = slot * 12 + g

        def body(n, state):
            for u in range(UNROLL):
                at = spread(n * UNROLL + u)
                v = proj[base + 4, at, :]
                state = ab[g] * state + v[None]
                proj[base + 8, at, :] = jnp.sum(wb[g] * state, axis=0) + bb[g] * v
            return state

        v = lax.fori_loop(0, STEPS // UNROLL, body, jnp.zeros((MODES, 8, 128), F32))
        step = jnp.exp(lb[g] * float(-STEPS))
        for d in (1, 2, 4):
            back = pltpu.roll(v, d, 1)
            v = v + jnp.where(lane8 >= d, step * back, 0.0)
            step = step * step
        xe[slot * LG + g] = jnp.where(lane8 >= 1, pltpu.roll(v, 1, 1), 0.0)
        for r in range(MODES):
            et[slot, g, pl.ds(r, 1), :] = v[r, 7:8, :]

    def filter_slot(slot):
        def body(g, _):
            fir(slot, g)
            scan(slot, g)
            return 0

        lax.fori_loop(0, LG, body, 0)

    for cp in win_copies:
        cp.wait()
    project_own(k)
    xz[1].wait_recv()
    xf[1].start()
    wbig = []
    for cp in wa:
        cp.wait_recv()
    line_a = pl.ds(pl.multiple_of(y * 64, 64), 64)
    line_b = pl.ds(pl.multiple_of(256 + x * 64, 64), 64)
    for i in range(3):
        wbig.append(remote(wo.at[far_j, line_a], wo.at[far_j, line_a], S_WB + i, y_peers[i]))
        wbig.append(remote(wo.at[far_j, line_b], wo.at[far_j, line_b], S_WB + 3 + i, x_peers[i]))
    for cp in wbig:
        cp.start()
    for c in ORDER:
        xd[c].wait_recv()
    project_own(1 - k)
    wd = remote(w_out, wo.at[own_j], S_WD, other)
    wd.start()
    filter_slot(k)
    xz[0].wait_recv()
    xf[0].start()
    filter_slot(1 - k)
    xf[1].wait_recv()
    project_far(1)
    xf[0].wait_recv()
    project_far(0)
    wc = remote(wo.at[far_j], wo.at[far_j], S_WC, other)
    for c in ORDER[2:]:
        xz[c].wait_recv()
        xf[c].start()
        if c == ORDER[-1]:
            for cp in wbig:
                cp.wait_recv()
            wc.start()
        xf[c].wait_recv()
        project_far(c)

    filter_slot(2)
    filter_slot(3)

    def power(n):
        return jnp.exp(lam[...] * (-float(ROWS) * n.astype(F32)))

    lam3 = lam[...]
    one = jnp.exp(lam3 * -float(ROWS))
    m0, m1, m2, sg = 2 * p, 1 - p, 3 - 2 * p, 2 + p
    r1[line_at, 0] = (et[m2] + one * (et[m1] + one * et[m0])).astype(STATE)
    r1[line_at, 1] = et[sg].astype(STATE)
    e1 = [remote(r1.at[line_at], r1.at[line_at], S_E1 + i, line_peers[i]) for i in range(7)]
    for cp in e1:
        cp.start()
    cm, cq = power(1 - p), power(3 * p)
    group = jnp.exp(lam3 * -float(4 * ROWS))
    line = jnp.exp(lam3 * -float(16 * ROWS))
    for cp in e1:
        cp.wait_recv()
    before, totals = [], []
    for hh in range(2):
        run = jnp.zeros((LG, MODES, 128), F32)
        pre = run
        for xx in range(4):
            pre = jnp.where(x == xx, run, pre)
            run = group * run + cm * r1[hh * 4 + xx, 0].astype(F32) + cq * r1[(1 - hh) * 4 + xx, 1].astype(F32)
        before.append(pre)
        r2[y, hh] = run.astype(STATE)
    e2 = [remote(r2.at[y], r2.at[y], S_E2 + i, y_peers[i]) for i in range(3)]
    for cp in e2:
        cp.start()
    to_x = power(4 * x)
    to_y = power(16 * y)
    for cp in e2:
        cp.wait_recv()
    into = []
    plane = None
    for hh in range(2):
        run = jnp.zeros((LG, MODES, 128), F32)
        pre = run
        for yy in range(4):
            pre = jnp.where(y == yy, run, pre)
            run = line * run + r2[yy, hh].astype(F32)
        if hh == 1:
            pre = pre + to_y * plane
        plane = run
        into.append(to_x * pre + before[hh])
    mine = jnp.where(h == 0, into[0], into[1])
    theirs = jnp.where(h == 0, into[1], into[0])
    far_at = lax.rem(line_at + 4, 8)
    pf = p.astype(F32)
    s_main = power(p) * mine + pf * r1[far_at, 1].astype(F32)
    s_single = power(3 * (1 - p)) * theirs + (1.0 - pf) * r1[far_at, 0].astype(F32)
    sin[m0] = s_main
    s_main = one * s_main + et[m0]
    sin[m1] = s_main
    sin[m2] = one * s_main + et[m1]
    sin[sg] = s_single

    piece = lax.broadcasted_iota(jnp.int32, (1, 8, 128), 1).astype(F32) * float(-STEPS)

    def finish(slot, dst):
        def per_group(g, _):
            base = slot * 12 + g
            came = jnp.stack([jnp.broadcast_to(sin[slot, g, pl.ds(r, 1), :], (8, 128)) for r in range(MODES)])
            state = wb[g] * (xe[slot * LG + g] + jnp.exp(lb[g] * piece) * came)

            def body(n, state):
                for u in range(UNROLL):
                    at = spread(n * UNROLL + u)
                    state = ab[g] * state
                    v = proj[base + 8, at, :] + jnp.sum(state, axis=0)
                    proj[base + 8, at, :] = proj[base, at, :] * v
                return state

            lax.fori_loop(0, STEPS // UNROLL, body, state)
            return 0

        lax.fori_loop(0, LG, per_group, 0)
        for g in range(LG):
            dst[:, pl.ds(g * 128, 128)] = proj[slot * 12 + 8 + g, pl.ds(HALO, ROWS), :].astype(BF)

    sends = []
    for i, (slot, to) in enumerate(((2 + k, partner), (3 - k, gate_to), (1 - k, other))):
        finish(slot, gs.at[i])
        cp = remote(gs.at[i], gg.at[own_j], S_G + i, to)
        cp.start()
        sends.append(cp)
    for c in ORDER:
        xz[c].wait_send()
        xd[c].wait_send()
    res_copy = local(tok, xo.at[k, pl.ds(HALO, ROWS)], L_RES)
    res_copy.start()
    finish(k, gg.at[own_j])

    wo_copy.wait()
    res_copy.wait()

    def out_pass(js, kind):
        def body(n, _):
            cols = pl.ds(pl.multiple_of(n * OUT_COLS, OUT_COLS), OUT_COLS)
            tiles = OUT_COLS // 128
            if kind == 0:
                v = xo[k, pl.ds(HALO, ROWS), cols].astype(F32)
            else:
                v = jnp.concatenate([proj[n * tiles + i, pl.ds(0, ROWS), :] for i in range(tiles)], axis=1)
            for j in js:
                v = v + jnp.dot(gg[j], wo[j, :, cols], preferred_element_type=F32)
            if kind == 2:
                xo[1 - k, pl.ds(0, ROWS), cols] = v.astype(BF)
                local(xo.at[1 - k, pl.ds(0, ROWS), cols], out.at[:, cols], L_OUT + n).start()
            else:
                for i in range(tiles):
                    proj[n * tiles + i, pl.ds(0, ROWS), :] = v[:, i * 128 : (i + 1) * 128]
            return 0

        lax.fori_loop(0, OUT_TILES, body, 0)

    wd.wait_recv()
    sends[2].wait_recv()
    out_pass((own_j, oth_j), 0)
    wc.wait_recv()
    sends[0].wait_recv()
    out_pass((far_j,), 1)
    sends[1].wait_recv()
    out_pass((far2_j,), 2)

    for cp in [halo_copy] + wz + wa + wbig + [wd, wc] + list(xf.values()) + e1 + e2 + sends:
        cp.wait_send()
    for n in range(OUT_TILES):
        cols = pl.ds(n * OUT_COLS, OUT_COLS)
        local(xo.at[1 - k, pl.ds(0, ROWS), cols], out.at[:, cols], L_OUT + n).wait()


def shards(tokens, norm_gain, w_in, short_weight, conv_bias, decay_rates, residues, w_out):
    vmem = pl.BlockSpec(memory_space=pltpu.VMEM)
    hbm = pl.BlockSpec(memory_space=pl.ANY)
    return pl.pallas_call(
        kernel,
        out_shape=jax.ShapeDtypeStruct((ROWS, WIDTH), BF),
        in_specs=[hbm, vmem, hbm, vmem, vmem, vmem, vmem, hbm],
        out_specs=hbm,
        scratch_shapes=[
            pltpu.VMEM((2, SLOT, WIDTH), BF),
            pltpu.VMEM((CHUNKS, 2, CROWS, WIDTH), BF),
            pltpu.VMEM((3, WIDTH, CH), BF),
            pltpu.VMEM((4, CH, WIDTH), BF),
            pltpu.VMEM((48, SLOT, 128), F32),
            pltpu.VMEM((3, ROWS, CH), BF),
            pltpu.VMEM((4, ROWS, CH), BF),
            pltpu.VMEM((LG, TAPS, 3, 8, 128), F32),
            pltpu.VMEM((LG, MODES, 8, 128), F32),
            pltpu.VMEM((LG, MODES, 8, 128), F32),
            pltpu.VMEM((LG, MODES, 8, 128), F32),
            pltpu.VMEM((LG, 8, 128), F32),
            pltpu.VMEM((LG, MODES, 128), F32),
            pltpu.VMEM((4 * LG, MODES, 8, 128), F32),
            pltpu.VMEM((4, LG, MODES, 128), F32),
            pltpu.VMEM((4, LG, MODES, 128), F32),
            pltpu.VMEM((8, 2, LG, MODES, 128), STATE),
            pltpu.VMEM((4, 2, LG, MODES, 128), STATE),
            pltpu.SemaphoreType.DMA((S_N,)),
            pltpu.SemaphoreType.DMA((S_N,)),
            pltpu.SemaphoreType.DMA((L_N,)),
        ],
        compiler_params=pltpu.CompilerParams(
            collective_id=0, has_side_effects=True, vmem_limit_bytes=60 * 2**20
        ),
        cost_estimate=pl.CostEstimate(flops=26 * 10**9, bytes_accessed=25 * 2**20, transcendentals=0),
    )(
        tokens,
        norm_gain.reshape(1, WIDTH),
        w_in.transpose(1, 0, 2),
        short_weight.transpose(1, 0, 2),
        conv_bias.reshape(1, CH),
        decay_rates,
        residues,
        w_out,
    )


def solution(mesh):
    in_specs = (
        P(("ctx", "tp"), None),
        P(),
        P(None, None, "tp"),
        P(None, None, "tp"),
        P("tp"),
        P(None, "tp"),
        P(None, "tp"),
        P("tp", None),
    )
    return jax.shard_map(
        shards, mesh=mesh, in_specs=in_specs, out_specs=P(("ctx", "tp"), None), check_vma=False
    )
```

```python
import functools

import jax
import jax.numpy as jnp
from jax import lax
from jax.experimental import pallas as pl
from jax.experimental.pallas import tpu as pltpu
from jax.sharding import PartitionSpec as P

MESH = pl.DeviceIdType.MESH
BF, F32 = jnp.bfloat16, jnp.float32
STATE = F32

ROWS = 384
HALO = 16
SLOT = ROWS + HALO
WIDTH = 4096
CH = 512
FIRST = (0, 112, 208, 304)
COUNT = (112, 96, 96, 96)
CHUNKS = 4
ORDER = (1, 0, 2, 3)
PARTS = ((0, 0, 112), (1, 0, 96), (2, 0, 96), (3, 0, 48), (3, 48, 48))
LATE = 96
EARLY = ROWS - LATE
PIECES = 8
MODES = 16
TAPS = 7
LG = CH // 128
UNROLL = 12

S_HALO = 0
S_XZ = 1
S_XD = S_XZ + len(PARTS)
S_XF = S_XD + len(PARTS)
S_WZ = S_XF + len(PARTS)
S_WD = S_WZ + 2
S_WA = S_WD + 1
S_WB = S_WA + 6
S_WC = S_WB + 6
S_EZ = S_WC + 1
S_EX = S_EZ + LG
S_EY = S_EX + 3 * LG
S_G = S_EY + 3 * LG
S_N = S_G + 3 * LG
L_TOK = 0
L_WIN = CHUNKS
L_WO = L_WIN + 3
L_RES = L_WO + 1
L_OUT = L_RES + 1
OUT_TILES = 4
L_N = L_OUT + OUT_TILES
OUT_COLS = WIDTH // OUT_TILES


def kernel(
    tok, gain, w3, taps, bias, decay, resid, w_out, out,
    xo, xr, wi, wo, proj, late, gs, gg, tapb, ab, wb, lb, bb, lam, xe, et, ea, sin, grow, bf, mq, rz, r1, r2, ss, rs, ls,
):
    ctx = lax.axis_index("ctx")
    tp = lax.axis_index("tp")
    x = lax.rem(ctx, 4)
    y = lax.rem(lax.div(ctx, 4), 4)
    h = lax.div(ctx, 16)
    p = lax.div(tp, 2)
    k = lax.rem(tp, 2)
    z = 2 * h + p
    s = 2 * k - 1

    def dev(dx, dy, dz, core):
        zz = lax.rem(dz + 4, 4)
        return (lax.div(zz, 2) * 16 + lax.rem(dy, 4) * 4 + lax.rem(dx, 4), lax.rem(zz, 2) * 2 + core)

    order_at = ctx * 4 + tp
    nxt = lax.rem(order_at + 1, 128)
    prv = lax.rem(order_at + 127, 128)
    nxt = (lax.div(nxt, 4), lax.rem(nxt, 4))
    prv = (lax.div(prv, 4), lax.rem(prv, 4))
    other = dev(x, y, z, 1 - k)
    partner = dev(x, y, z + s, 1 - k)
    gate_to = dev(x, y, z - s, k)
    gate_from = dev(x, y, z + s, k)
    x_peers = [dev(x + d, y, z, k) for d in (1, 2, 3)]
    y_peers = [dev(x, y + d, z, k) for d in (1, 2, 3)]
    mirror = dev(x, y, z + 2, k)
    own_j = 2 * p + k
    oth_j = 2 * p + 1 - k
    far_j = 2 * (1 - p) + 1 - k
    far2_j = 2 * (1 - p) + k

    def remote(src, dst, at, to):
        return pltpu.make_async_remote_copy(
            src_ref=src, dst_ref=dst, send_sem=ss.at[at], recv_sem=rs.at[at], device_id=to, device_id_type=MESH
        )

    def local(src, dst, at):
        return pltpu.make_async_copy(src, dst, ls.at[at])

    tok_copies = {}
    for c in ORDER:
        to = max(FIRST[c], HALO)
        count = FIRST[c] + COUNT[c] - to
        tok_copies[c] = local(tok.at[pl.ds(to - HALO, count)], xo.at[k, pl.ds(to, count)], L_TOK + c)
        tok_copies[c].start()
    win_copies = [local(w3.at[i], wi.at[i], L_WIN + i) for i in range(3)]
    for cp in win_copies:
        cp.start()
    wo_copy = local(w_out, wo.at[own_j], L_WO)

    barrier = pltpu.get_barrier_semaphore()
    greet = [nxt, prv, other, partner, gate_to, gate_from, mirror] + x_peers + y_peers
    for to in greet:
        pl.semaphore_signal(barrier, inc=1, device_id=to, device_id_type=MESH)
    pl.semaphore_wait(barrier, len(greet))

    halo_copy = remote(tok.at[pl.ds(ROWS - HALO, HALO)], xo.at[1 - k, pl.ds(0, HALO)], S_HALO, nxt)
    halo_copy.start()
    row_a = pl.multiple_of((y * 4 + x) * 16, 16)
    row_b = pl.multiple_of(256 + (x * 4 + y) * 16, 16)
    wz = [
        remote(w_out.at[pl.ds(r, 16)], wo.at[own_j, pl.ds(r, 16)], S_WZ + i, partner)
        for i, r in enumerate((row_a, row_b))
    ]
    for cp in wz:
        cp.start()

    for i in range(WIDTH // 128):
        grow[:, i * 128 : (i + 1) * 128] = gain[i : i + 1, :].astype(F32)

    def norm_rows(first, count):
        def body(i, _):
            at = pl.ds(pl.multiple_of(first + i * 16, 16), 16)
            v = xo[k, at, :].astype(F32)
            total = v[:, :128] * v[:, :128]
            for n in range(1, WIDTH // 128):
                total = total + v[:, n * 128 : (n + 1) * 128] * v[:, n * 128 : (n + 1) * 128]
            scale = lax.rsqrt(jnp.sum(total, axis=1, keepdims=True) * (1.0 / WIDTH) + 1e-6)
            xo[k, at, :] = (v * scale * grow[...]).astype(BF)
            return 0

        lax.fori_loop(0, count // 16, body, 0)

    xz, xd, xf = {}, {}, {}
    for c in ORDER:
        tok_copies[c].wait()
        if c == 0:
            halo_copy.wait_recv()

            @pl.when(order_at == 0)
            def _():
                xo[k, pl.ds(0, HALO), :] = jnp.zeros((HALO, WIDTH), BF)

        norm_rows(FIRST[c], COUNT[c])
        for at, (chunk, off, count) in enumerate(PARTS):
            if chunk != c:
                continue

            def landed(core):
                row = 2 * FIRST[c] + core * COUNT[c] + off
                return xr.at[pl.ds(pl.multiple_of(row, 16), count)]

            part = xo.at[k, pl.ds(FIRST[c] + off, count)]
            xz[at] = remote(part, landed(1 - k), S_XZ + at, partner)
            xz[at].start()
            xd[at] = remote(part, part, S_XD + at, other)
            xd[at].start()
            xf[at] = remote(landed(k), landed(k), S_XF + at, other)

    for cp in wz:
        cp.wait_recv()
    wa, wbig = [], []
    for i in range(3):
        wa.append(remote(wo.at[far_j, pl.ds(row_a, 16)], wo.at[far_j, pl.ds(row_a, 16)], S_WA + i, x_peers[i]))
        wa.append(remote(wo.at[far_j, pl.ds(row_b, 16)], wo.at[far_j, pl.ds(row_b, 16)], S_WA + 3 + i, y_peers[i]))
    for cp in wa:
        cp.start()

    rate = decay[...]
    weight = resid[...] * jnp.sqrt(2.0 * rate)
    fall = jnp.exp(-rate)
    tap_rows = taps[...].astype(F32)
    for g in range(LG):
        cols = slice(g * 128, (g + 1) * 128)
        lam[g] = rate[:, cols]
        bb[g] = jnp.broadcast_to(bias[:, cols], (8, 128))
        for r in range(MODES):
            lb[g, r] = jnp.broadcast_to(rate[r : r + 1, cols], (8, 128))
            ab[g, r] = jnp.broadcast_to(fall[r : r + 1, cols], (8, 128))
            wb[g, r] = jnp.broadcast_to(weight[r : r + 1, cols], (8, 128))
        for j in range(TAPS):
            for i in range(3):
                tapb[g, j, i] = jnp.broadcast_to(tap_rows[i, j : j + 1, cols], (8, 128))

    def project_own(slot):
        def body(n, _):
            v = jnp.dot(xo[slot], wi[n], preferred_element_type=F32)
            for b in range(4):
                proj[slot * 12 + 4 * n + b] = v[:, b * 128 : (b + 1) * 128]
            return 0

        lax.fori_loop(0, 3, body, 0, unroll=3)

    def project_far(c):
        first, count = FIRST[c], COUNT[c]

        def body(n, _):
            v = jnp.dot(xr[pl.ds(2 * first, 2 * count)], wi[n], preferred_element_type=F32)
            for a in range(2):
                for b in range(4):
                    part = v[a * count : (a + 1) * count, b * 128 : (b + 1) * 128]
                    if c < CHUNKS - 1:
                        proj[(2 + a) * 12 + 4 * n + b, pl.ds(first, count)] = part
                    else:
                        late[a * 12 + 4 * n + b, pl.ds(HALO, LATE)] = part
                    if c == CHUNKS - 2:
                        late[a * 12 + 4 * n + b, pl.ds(0, HALO)] = part[count - HALO :]
            return 0

        lax.fori_loop(0, 3, body, 0)

    def spread(steps, i):
        return pl.ds(HALO + i, PIECES, stride=steps)

    def fir(ref, base, steps, g, streams):
        base = base + g

        def body(n, past):
            places = [spread(steps, n * UNROLL + u) for u in range(UNROLL)]
            fresh = [[ref[base + 4 * i, at, :] for at in places] for i in streams]
            rows = [list(old) + new for old, new in zip(past, fresh)]
            totals = []
            for i, row in zip(streams, rows):
                stream = []
                for u in range(UNROLL):
                    t = [tapb[g, j, i] * row[u + TAPS - 1 - j] for j in range(TAPS)]
                    stream.append(((t[0] + t[1]) + (t[2] + t[3])) + ((t[4] + t[5]) + t[6]))
                totals.append(stream)
            for u, at in enumerate(places):
                if streams == (0,):
                    ref[base, at, :] = totals[0][u]
                else:
                    ref[base + 4, at, :] = totals[0][u] * totals[1][u]
            return tuple(tuple(row[UNROLL:]) for row in rows)

        past = tuple(
            tuple(ref[base + 4 * i, spread(steps, m - (TAPS - 1)), :] for m in range(TAPS - 1)) for i in streams
        )
        lax.fori_loop(0, steps // UNROLL, body, past)

    lane8 = lax.broadcasted_iota(jnp.int32, (1, 8, 128), 1)

    def mode_sum(v):
        count = MODES
        while count > 1:
            count //= 2
            v = v[:count] + v[count:]
        return v[0]

    def scan(ref, base, steps, unit, g, outputs, ends):
        base = base + g

        def body(n, state):
            places = [spread(steps, n * UNROLL + u) for u in range(UNROLL)]
            values = [ref[base + 4, at, :] for at in places]
            sums = []
            for v in values:
                state = ab[g] * state + v[None]
                if outputs:
                    sums.append(mode_sum(wb[g] * state) + bb[g] * v)
            for at, v in zip(places, sums):
                ref[base + 8, at, :] = v
            return state

        v = lax.fori_loop(0, steps // UNROLL, body, jnp.zeros((MODES, 8, 128), F32))
        if not ends:
            return
        step = jnp.exp(lb[g] * float(-steps))
        for d in (1, 2, 4):
            back = pltpu.roll(v, d, 1)
            v = v + jnp.where(lane8 >= d, step * back, 0.0)
            step = step * step
        xe[unit * LG + g] = jnp.where(lane8 >= 1, pltpu.roll(v, 1, 1), 0.0)
        for r in range(MODES):
            et[unit, g, pl.ds(r, 1), :] = v[r, 7:8, :]

    def filter_own(slot):
        def body(g, _):
            fir(proj, slot * 12, ROWS // PIECES, g, (1, 2))
            scan(proj, slot * 12, ROWS // PIECES, slot, g, True, True)
            fir(proj, slot * 12, ROWS // PIECES, g, (0,))
            return 0

        lax.fori_loop(0, LG, body, 0)

    def filter_early():
        def body(n, _):
            i, g = lax.div(n, LG), lax.rem(n, LG)
            fir(proj, 24 + i * 12, EARLY // PIECES, g, (1, 2))
            scan(proj, 24 + i * 12, EARLY // PIECES, 2 + i, g, False, True)
            return 0

        lax.fori_loop(0, 2 * LG, body, 0)

    def filter_late(g):
        for i in range(2):
            fir(late, i * 12, LATE // PIECES, g, (1, 2))
            scan(late, i * 12, LATE // PIECES, 4 + i, g, False, True)

    def filter_rest(g):
        def body(i, _):
            fir(proj, 24 + i * 12, EARLY // PIECES, g, (0,))
            scan(proj, 24 + i * 12, EARLY // PIECES, 0, g, True, False)
            fir(late, i * 12, LATE // PIECES, g, (0,))
            scan(late, i * 12, LATE // PIECES, 0, g, True, False)
            return 0

        lax.fori_loop(0, 2, body, 0)

    for cp in win_copies:
        cp.wait()
    wo_copy.start()
    project_own(k)
    xz[1].wait_recv()
    xf[1].start()
    wbig = []
    for cp in wa:
        cp.wait_recv()
    line_a = pl.ds(pl.multiple_of(y * 64, 64), 64)
    line_b = pl.ds(pl.multiple_of(256 + x * 64, 64), 64)
    for i in range(3):
        wbig.append(remote(wo.at[far_j, line_a], wo.at[far_j, line_a], S_WB + i, y_peers[i]))
        wbig.append(remote(wo.at[far_j, line_b], wo.at[far_j, line_b], S_WB + 3 + i, x_peers[i]))
    for cp in wbig:
        cp.start()
    for at in xd:
        xd[at].wait_recv()
    project_own(1 - k)
    wd = remote(w_out, wo.at[own_j], S_WD, other)
    wd.start()
    xf[1].wait_recv()
    project_far(1)
    filter_own(k)
    xz[0].wait_recv()
    xf[0].start()
    xf[0].wait_recv()
    project_far(0)
    filter_own(1 - k)
    xz[2].wait_recv()
    xf[2].start()
    xf[2].wait_recv()
    project_far(2)
    filter_early()
    wc = remote(wo.at[far_j], wo.at[far_j], S_WC, other)
    for at in (3, 4):
        xz[at].wait_recv()
        xf[at].start()
    for at in (3, 4):
        xf[at].wait_recv()
    project_far(3)

    m0, m1, m2, sg = 2 * p, 1 - p, 3 - 2 * p, 2 + p
    ez, ex, ey, sends = {}, {}, {}, {}

    def power(g, n):
        return jnp.exp(lam[g] * (-float(ROWS) * jnp.asarray(n).astype(F32)))

    def fall_over(g, tokens):
        return jnp.exp(lam[g] * -float(tokens))

    def send_z(g):
        one = power(g, 1)
        for i in range(2):
            ea[i, g] = et[2 + i, g]
            et[2 + i, g] = fall_over(g, LATE) * et[2 + i, g] + et[4 + i, g]
        mq[g, 0] = (et[m2, g] + one * (et[m1, g] + one * et[m0, g])).astype(STATE)
        mq[g, 1] = et[sg, g].astype(STATE)
        ez[g] = remote(mq.at[g], rz.at[g], S_EZ + g, mirror)
        ez[g].start()

    def send_x(g):
        cm, cq = power(g, 1 - p), power(g, 3 * p)
        ez[g].wait_recv()
        own, far = mq[g].astype(F32), rz[g].astype(F32)
        r1[g, x, h] = (cm * own[0] + cq * far[1]).astype(STATE)
        r1[g, x, 1 - h] = (cm * far[0] + cq * own[1]).astype(STATE)
        ex[g] = [remote(r1.at[g, x], r1.at[g, x], S_EX + 3 * g + i, x_peers[i]) for i in range(3)]
        for cp in ex[g]:
            cp.start()

    def send_y(g):
        group = power(g, 4)
        for cp in ex[g]:
            cp.wait_recv()
        for hh in range(2):
            run = jnp.zeros((MODES, 128), F32)
            pre = run
            for xx in range(4):
                pre = jnp.where(x == xx, run, pre)
                run = group * run + r1[g, xx, hh].astype(F32)
            bf[g, hh] = pre
            r2[g, y, hh] = run.astype(STATE)
        ey[g] = [remote(r2.at[g, y], r2.at[g, y], S_EY + 3 * g + i, y_peers[i]) for i in range(3)]
        for cp in ey[g]:
            cp.start()

    def states(g):
        line = power(g, 16)
        to_x = power(g, 4 * x)
        to_y = power(g, 16 * y)
        one = power(g, 1)
        for cp in ey[g]:
            cp.wait_recv()
        into = []
        plane = None
        for hh in range(2):
            run = jnp.zeros((MODES, 128), F32)
            pre = run
            for yy in range(4):
                pre = jnp.where(y == yy, run, pre)
                run = line * run + r2[g, yy, hh].astype(F32)
            if hh == 1:
                pre = pre + to_y * plane
            plane = run
            into.append(to_x * pre + bf[g, hh])
        mine = jnp.where(h == 0, into[0], into[1])
        theirs = jnp.where(h == 0, into[1], into[0])
        pf = p.astype(F32)
        s_main = power(g, p) * mine + pf * rz[g, 1].astype(F32)
        sin[sg, g] = power(g, 3 * (1 - p)) * theirs + (1.0 - pf) * rz[g, 0].astype(F32)
        sin[m0, g] = s_main
        s_main = one * s_main + et[m0, g]
        sin[m1, g] = s_main
        sin[m2, g] = one * s_main + et[m1, g]
        for i in range(2):
            sin[4 + i, g] = fall_over(g, EARLY) * sin[2 + i, g] + ea[i, g]

    piece = lax.broadcasted_iota(jnp.int32, (1, 8, 128), 1).astype(F32)

    def finish_part(ref, base, steps, unit, g, dst, first):
        base = base + g
        came = jnp.stack([jnp.broadcast_to(sin[unit, g, pl.ds(r, 1), :], (8, 128)) for r in range(MODES)])
        state = wb[g] * (xe[unit * LG + g] + jnp.exp(lb[g] * piece * float(-steps)) * came)

        def body(n, state):
            places = [spread(steps, n * UNROLL + u) for u in range(UNROLL)]
            values = [(ref[base, at, :], ref[base + 8, at, :]) for at in places]
            gated = []
            for q, v in values:
                state = ab[g] * state
                gated.append(q * (v + mode_sum(state)))
            for at, v in zip(places, gated):
                ref[base + 8, at, :] = v
            return state

        lax.fori_loop(0, steps // UNROLL, body, state)
        dst[pl.ds(first, PIECES * steps), :] = ref[base + 8, pl.ds(HALO, PIECES * steps), :].astype(BF)

    def finish(slot, g, dst, far):
        if far:
            finish_part(proj, slot * 12, EARLY // PIECES, slot, g, dst, 0)
            finish_part(late, (slot - 2) * 12, LATE // PIECES, slot + 2, g, dst, EARLY)
        else:
            finish_part(proj, slot * 12, ROWS // PIECES, slot, g, dst, 0)

    def finish_all(g):
        for i, (slot, to) in enumerate(((2 + k, partner), (3 - k, gate_to), (1 - k, other))):
            finish(slot, g, gs.at[i, g], i < 2)
            sends[i, g] = remote(gs.at[i, g], gg.at[own_j, g], S_G + 3 * g + i, to)
            sends[i, g].start()
        finish(k, g, gg.at[own_j, g], False)

    for g in range(LG):
        filter_late(g)
        send_z(g)
    for cp in wbig:
        cp.wait_recv()
    wc.start()
    filter_rest(0)
    for g in range(LG):
        send_x(g)
    filter_rest(1)
    for g in range(LG):
        send_y(g)
    filter_rest(2)
    states(0)
    finish_all(0)
    filter_rest(3)
    for at in xz:
        xz[at].wait_send()
        xd[at].wait_send()
    res_copy = local(tok, xo.at[k, pl.ds(HALO, ROWS)], L_RES)
    res_copy.start()
    for g in range(1, LG):
        states(g)
        finish_all(g)

    wo_copy.wait()
    res_copy.wait()

    def out_pass(js, halves, kind):
        def body(n, _):
            cols = pl.ds(pl.multiple_of(n * OUT_COLS, OUT_COLS), OUT_COLS)
            tiles = OUT_COLS // 128
            if kind == 0:
                v = xo[k, pl.ds(HALO, ROWS), cols].astype(F32)
            else:
                v = jnp.concatenate([proj[n * tiles + i, pl.ds(0, ROWS), :] for i in range(tiles)], axis=1)
            for j in js:
                for half in halves:
                    lhs = jnp.concatenate([gg[j, 2 * half], gg[j, 2 * half + 1]], axis=1)
                    rows = slice(half * 256, half * 256 + 256)
                    v = v + jnp.dot(lhs, wo[j, rows, cols], preferred_element_type=F32)
            if kind == 2:
                xo[1 - k, pl.ds(0, ROWS), cols] = v.astype(BF)
                local(xo.at[1 - k, pl.ds(0, ROWS), cols], out.at[:, cols], L_OUT + n).start()
            else:
                for i in range(tiles):
                    proj[n * tiles + i, pl.ds(0, ROWS), :] = v[:, i * 128 : (i + 1) * 128]
            return 0

        lax.fori_loop(0, OUT_TILES, body, 0)

    wd.wait_recv()
    for g in range(LG):
        sends[2, g].wait_recv()
    out_pass((own_j, oth_j), (0, 1), 0)
    wc.wait_recv()
    for half in (0, 1):
        for g in (2 * half, 2 * half + 1):
            for i in range(2):
                sends[i, g].wait_recv()
        out_pass((far_j, far2_j), (half,), 1 + half)

    for cp in [halo_copy] + wz + wa + wbig + [wd, wc] + list(xf.values()) + list(ez.values()) + list(sends.values()):
        cp.wait_send()
    for g in range(LG):
        for cp in ex[g] + ey[g]:
            cp.wait_send()
    for n in range(OUT_TILES):
        cols = pl.ds(n * OUT_COLS, OUT_COLS)
        local(xo.at[1 - k, pl.ds(0, ROWS), cols], out.at[:, cols], L_OUT + n).wait()


def shards(tokens, norm_gain, w_in, short_weight, conv_bias, decay_rates, residues, w_out):
    vmem = pl.BlockSpec(memory_space=pltpu.VMEM)
    hbm = pl.BlockSpec(memory_space=pl.ANY)
    return pl.pallas_call(
        kernel,
        out_shape=jax.ShapeDtypeStruct((ROWS, WIDTH), BF),
        in_specs=[hbm, vmem, hbm, vmem, vmem, vmem, vmem, hbm],
        out_specs=hbm,
        scratch_shapes=[
            pltpu.VMEM((2, SLOT, WIDTH), BF),
            pltpu.VMEM((2 * SLOT, WIDTH), BF),
            pltpu.VMEM((3, WIDTH, CH), BF),
            pltpu.VMEM((4, CH, WIDTH), BF),
            pltpu.VMEM((48, SLOT, 128), F32),
            pltpu.VMEM((24, HALO + LATE, 128), F32),
            pltpu.VMEM((3, LG, ROWS, 128), BF),
            pltpu.VMEM((4, LG, ROWS, 128), BF),
            pltpu.VMEM((LG, TAPS, 3, 8, 128), F32),
            pltpu.VMEM((LG, MODES, 8, 128), F32),
            pltpu.VMEM((LG, MODES, 8, 128), F32),
            pltpu.VMEM((LG, MODES, 8, 128), F32),
            pltpu.VMEM((LG, 8, 128), F32),
            pltpu.VMEM((LG, MODES, 128), F32),
            pltpu.VMEM((6 * LG, MODES, 8, 128), F32),
            pltpu.VMEM((6, LG, MODES, 128), F32),
            pltpu.VMEM((2, LG, MODES, 128), F32),
            pltpu.VMEM((6, LG, MODES, 128), F32),
            pltpu.VMEM((1, WIDTH), F32),
            pltpu.VMEM((LG, 2, MODES, 128), F32),
            pltpu.VMEM((LG, 2, MODES, 128), STATE),
            pltpu.VMEM((LG, 2, MODES, 128), STATE),
            pltpu.VMEM((LG, 4, 2, MODES, 128), STATE),
            pltpu.VMEM((LG, 4, 2, MODES, 128), STATE),
            pltpu.SemaphoreType.DMA((S_N,)),
            pltpu.SemaphoreType.DMA((S_N,)),
            pltpu.SemaphoreType.DMA((L_N,)),
        ],
        compiler_params=pltpu.CompilerParams(
            collective_id=0, has_side_effects=True, vmem_limit_bytes=60 * 2**20
        ),
        cost_estimate=pl.CostEstimate(flops=26 * 10**9, bytes_accessed=25 * 2**20, transcendentals=0),
    )(
        tokens,
        norm_gain.reshape(WIDTH // 128, 128),
        w_in.transpose(1, 0, 2),
        short_weight.transpose(1, 0, 2),
        conv_bias.reshape(1, CH),
        decay_rates,
        residues,
        w_out,
    )


def solution(mesh):
    in_specs = (
        P(("ctx", "tp"), None),
        P(),
        P(None, None, "tp"),
        P(None, None, "tp"),
        P("tp"),
        P(None, "tp"),
        P(None, "tp"),
        P("tp", None),
    )
    return jax.shard_map(
        shards, mesh=mesh, in_specs=in_specs, out_specs=P(("ctx", "tp"), None), check_vma=False
    )
```

```python
import functools

import jax
import jax.numpy as jnp
from jax import lax
from jax.experimental import pallas as pl
from jax.experimental.pallas import tpu as pltpu
from jax.sharding import PartitionSpec as P

MESH = pl.DeviceIdType.MESH
BF, F32 = jnp.bfloat16, jnp.float32
STATE = F32

ROWS = 384
HALO = 16
SLOT = ROWS + HALO
WIDTH = 4096
CH = 512
FIRST = (0, 112, 208, 304)
COUNT = (112, 96, 96, 96)
CHUNKS = 4
ORDER = (1, 0, 2, 3)
PARTS = ((0, 0, 112), (1, 0, 96), (2, 0, 96), (3, 0, 48), (3, 48, 48))
LATE = 96
EARLY = ROWS - LATE
PIECES = 8
MODES = 16
TAPS = 7
LG = CH // 128
UNROLL = 12

S_HALO = 0
S_XZ = 1
S_XD = S_XZ + len(PARTS)
S_XF = S_XD + len(PARTS)
S_WZ = S_XF + len(PARTS)
S_WD = S_WZ + 2
S_WA = S_WD + 1
S_WB = S_WA + 6
S_WC = S_WB + 6
S_EZ = S_WC + 1
S_EX = S_EZ + LG
S_EY = S_EX + 3 * LG
S_G = S_EY + 3 * LG
S_N = S_G + 3 * LG
L_TOK = 0
L_WIN = CHUNKS
L_WO = L_WIN + 3
L_RES = L_WO + 1
L_OUT = L_RES + 1
OUT_TILES = 4
L_N = L_OUT + OUT_TILES
OUT_COLS = WIDTH // OUT_TILES


def kernel(
    tok, gain, w3, taps, bias, decay, resid, w_out, out,
    xo, xr, wi, wo, proj, late, gs, gg, tapb, ab, wb, lb, bb, lam, xe, et, ea, sin, grow, bf, mq, rz, r1, r2, ss, rs, ls,
):
    ctx = lax.axis_index("ctx")
    tp = lax.axis_index("tp")
    x = lax.rem(ctx, 4)
    y = lax.rem(lax.div(ctx, 4), 4)
    h = lax.div(ctx, 16)
    p = lax.div(tp, 2)
    k = lax.rem(tp, 2)
    z = 2 * h + p
    s = 2 * k - 1

    def dev(dx, dy, dz, core):
        zz = lax.rem(dz + 4, 4)
        return (lax.div(zz, 2) * 16 + lax.rem(dy, 4) * 4 + lax.rem(dx, 4), lax.rem(zz, 2) * 2 + core)

    order_at = ctx * 4 + tp
    nxt = lax.rem(order_at + 1, 128)
    prv = lax.rem(order_at + 127, 128)
    nxt = (lax.div(nxt, 4), lax.rem(nxt, 4))
    prv = (lax.div(prv, 4), lax.rem(prv, 4))
    other = dev(x, y, z, 1 - k)
    partner = dev(x, y, z + s, 1 - k)
    gate_to = dev(x, y, z - s, k)
    gate_from = dev(x, y, z + s, k)
    x_peers = [dev(x + d, y, z, k) for d in (1, 2, 3)]
    y_peers = [dev(x, y + d, z, k) for d in (1, 2, 3)]
    mirror = dev(x, y, z + 2, k)
    own_j = 2 * p + k
    oth_j = 2 * p + 1 - k
    far_j = 2 * (1 - p) + 1 - k
    far2_j = 2 * (1 - p) + k

    def remote(src, dst, at, to):
        return pltpu.make_async_remote_copy(
            src_ref=src, dst_ref=dst, send_sem=ss.at[at], recv_sem=rs.at[at], device_id=to, device_id_type=MESH
        )

    def local(src, dst, at):
        return pltpu.make_async_copy(src, dst, ls.at[at])

    tok_copies = {}
    for c in ORDER:
        to = max(FIRST[c], HALO)
        count = FIRST[c] + COUNT[c] - to
        tok_copies[c] = local(tok.at[pl.ds(to - HALO, count)], xo.at[k, pl.ds(to, count)], L_TOK + c)
        tok_copies[c].start()
    win_copies = [local(w3.at[i], wi.at[i], L_WIN + i) for i in range(3)]
    for cp in win_copies:
        cp.start()
    wo_copy = local(w_out, wo.at[own_j], L_WO)

    barrier = pltpu.get_barrier_semaphore()
    greet = [nxt, prv, other, partner, gate_to, gate_from, mirror] + x_peers + y_peers
    for to in greet:
        pl.semaphore_signal(barrier, inc=1, device_id=to, device_id_type=MESH)
    pl.semaphore_wait(barrier, len(greet))

    halo_copy = remote(tok.at[pl.ds(ROWS - HALO, HALO)], xo.at[1 - k, pl.ds(0, HALO)], S_HALO, nxt)
    halo_copy.start()
    row_a = pl.multiple_of((y * 4 + x) * 16, 16)
    row_b = pl.multiple_of(256 + (x * 4 + y) * 16, 16)
    wz = [
        remote(w_out.at[pl.ds(r, 16)], wo.at[own_j, pl.ds(r, 16)], S_WZ + i, partner)
        for i, r in enumerate((row_a, row_b))
    ]
    for cp in wz:
        cp.start()

    for i in range(WIDTH // 128):
        grow[:, i * 128 : (i + 1) * 128] = gain[i : i + 1, :].astype(F32)

    def norm_rows(first, count):
        def body(i, _):
            at = pl.ds(pl.multiple_of(first + i * 16, 16), 16)
            v = xo[k, at, :].astype(F32)
            total = v[:, :128] * v[:, :128]
            for n in range(1, WIDTH // 128):
                total = total + v[:, n * 128 : (n + 1) * 128] * v[:, n * 128 : (n + 1) * 128]
            scale = lax.rsqrt(jnp.sum(total, axis=1, keepdims=True) * (1.0 / WIDTH) + 1e-6)
            xo[k, at, :] = (v * scale * grow[...]).astype(BF)
            return 0

        lax.fori_loop(0, count // 16, body, 0)

    xz, xd, xf = {}, {}, {}
    for c in ORDER:
        tok_copies[c].wait()
        if c == 0:
            halo_copy.wait_recv()

            @pl.when(order_at == 0)
            def _():
                xo[k, pl.ds(0, HALO), :] = jnp.zeros((HALO, WIDTH), BF)

        norm_rows(FIRST[c], COUNT[c])
        for at, (chunk, off, count) in enumerate(PARTS):
            if chunk != c:
                continue

            def landed(core):
                row = 2 * FIRST[c] + core * COUNT[c] + off
                return xr.at[pl.ds(pl.multiple_of(row, 16), count)]

            part = xo.at[k, pl.ds(FIRST[c] + off, count)]
            xz[at] = remote(part, landed(1 - k), S_XZ + at, partner)
            xz[at].start()
            xd[at] = remote(part, part, S_XD + at, other)
            xd[at].start()
            xf[at] = remote(landed(k), landed(k), S_XF + at, other)

    for cp in wz:
        cp.wait_recv()
    wa, wbig = [], []
    for i in range(3):
        wa.append(remote(wo.at[far_j, pl.ds(row_a, 16)], wo.at[far_j, pl.ds(row_a, 16)], S_WA + i, x_peers[i]))
        wa.append(remote(wo.at[far_j, pl.ds(row_b, 16)], wo.at[far_j, pl.ds(row_b, 16)], S_WA + 3 + i, y_peers[i]))
    for cp in wa:
        cp.start()

    rate = decay[...]
    weight = resid[...] * jnp.sqrt(2.0 * rate)
    fall = jnp.exp(-rate)
    tap_rows = taps[...].astype(F32)
    for g in range(LG):
        cols = slice(g * 128, (g + 1) * 128)
        lam[g] = rate[:, cols]
        bb[g] = jnp.broadcast_to(bias[:, cols], (8, 128))
        for r in range(MODES):
            lb[g, r] = jnp.broadcast_to(rate[r : r + 1, cols], (8, 128))
            ab[g, r] = jnp.broadcast_to(fall[r : r + 1, cols], (8, 128))
            wb[g, r] = jnp.broadcast_to(weight[r : r + 1, cols], (8, 128))
        for j in range(TAPS):
            for i in range(3):
                tapb[g, j, i] = jnp.broadcast_to(tap_rows[i, j : j + 1, cols], (8, 128))

    def project_own(slot):
        def body(n, _):
            v = jnp.dot(xo[slot], wi[n], preferred_element_type=F32)
            for b in range(4):
                proj[slot * 12 + 4 * n + b] = v[:, b * 128 : (b + 1) * 128]
            return 0

        lax.fori_loop(0, 3, body, 0, unroll=3)

    def project_far(c):
        first, count = FIRST[c], COUNT[c]

        def body(n, _):
            v = jnp.dot(xr[pl.ds(2 * first, 2 * count)], wi[n], preferred_element_type=F32)
            for a in range(2):
                for b in range(4):
                    part = v[a * count : (a + 1) * count, b * 128 : (b + 1) * 128]
                    if c < CHUNKS - 1:
                        proj[(2 + a) * 12 + 4 * n + b, pl.ds(first, count)] = part
                    else:
                        late[a * 12 + 4 * n + b, pl.ds(HALO, LATE)] = part
                    if c == CHUNKS - 2:
                        late[a * 12 + 4 * n + b, pl.ds(0, HALO)] = part[count - HALO :]
            return 0

        lax.fori_loop(0, 3, body, 0)

    def spread(steps, i):
        return pl.ds(HALO + i, PIECES, stride=steps)

    def fir(ref, base, steps, g, streams):
        base = base + g

        def body(n, past):
            places = [spread(steps, n * UNROLL + u) for u in range(UNROLL)]
            fresh = [[ref[base + 4 * i, at, :] for at in places] for i in streams]
            rows = [list(old) + new for old, new in zip(past, fresh)]
            totals = []
            for i, row in zip(streams, rows):
                stream = []
                for u in range(UNROLL):
                    t = [tapb[g, j, i] * row[u + TAPS - 1 - j] for j in range(TAPS)]
                    stream.append(((t[0] + t[1]) + (t[2] + t[3])) + ((t[4] + t[5]) + t[6]))
                totals.append(stream)
            for u, at in enumerate(places):
                if streams == (0,):
                    ref[base, at, :] = totals[0][u]
                else:
                    ref[base + 4, at, :] = totals[0][u] * totals[1][u]
            return tuple(tuple(row[UNROLL:]) for row in rows)

        past = tuple(
            tuple(ref[base + 4 * i, spread(steps, m - (TAPS - 1)), :] for m in range(TAPS - 1)) for i in streams
        )
        lax.fori_loop(0, steps // UNROLL, body, past)

    lane8 = lax.broadcasted_iota(jnp.int32, (1, 8, 128), 1)

    def mode_sum(v):
        count = MODES
        while count > 1:
            count //= 2
            v = v[:count] + v[count:]
        return v[0]

    def scan(ref, base, steps, unit, g, outputs, ends):
        base = base + g

        def body(n, state):
            places = [spread(steps, n * UNROLL + u) for u in range(UNROLL)]
            values = [ref[base + 4, at, :] for at in places]
            sums = []
            for v in values:
                state = ab[g] * state + v[None]
                if outputs:
                    sums.append(mode_sum(wb[g] * state) + bb[g] * v)
            for at, v in zip(places, sums):
                ref[base + 8, at, :] = v
            return state

        v = lax.fori_loop(0, steps // UNROLL, body, jnp.zeros((MODES, 8, 128), F32))
        if not ends:
            return
        step = jnp.exp(lb[g] * float(-steps))
        for d in (1, 2, 4):
            back = pltpu.roll(v, d, 1)
            v = v + jnp.where(lane8 >= d, step * back, 0.0)
            step = step * step
        xe[unit * LG + g] = jnp.where(lane8 >= 1, pltpu.roll(v, 1, 1), 0.0)
        for r in range(MODES):
            et[unit, g, pl.ds(r, 1), :] = v[r, 7:8, :]

    def filter_own(slot):
        def body(g, _):
            fir(proj, slot * 12, ROWS // PIECES, g, (1, 2))
            scan(proj, slot * 12, ROWS // PIECES, slot, g, True, True)
            fir(proj, slot * 12, ROWS // PIECES, g, (0,))
            return 0

        lax.fori_loop(0, LG, body, 0)

    def filter_early():
        def body(n, _):
            i, g = lax.div(n, LG), lax.rem(n, LG)
            fir(proj, 24 + i * 12, EARLY // PIECES, g, (1, 2))
            scan(proj, 24 + i * 12, EARLY // PIECES, 2 + i, g, False, True)
            return 0

        lax.fori_loop(0, 2 * LG, body, 0)

    def filter_late(g):
        for i in range(2):
            fir(late, i * 12, LATE // PIECES, g, (1, 2))
            scan(late, i * 12, LATE // PIECES, 4 + i, g, False, True)

    def filter_rest(g):
        def body(i, _):
            fir(proj, 24 + i * 12, EARLY // PIECES, g, (0,))
            scan(proj, 24 + i * 12, EARLY // PIECES, 0, g, True, False)
            fir(late, i * 12, LATE // PIECES, g, (0,))
            scan(late, i * 12, LATE // PIECES, 0, g, True, False)
            return 0

        lax.fori_loop(0, 2, body, 0)

    for cp in win_copies:
        cp.wait()
    wo_copy.start()
    project_own(k)
    xz[1].wait_recv()
    xf[1].start()
    wbig = []
    for cp in wa:
        cp.wait_recv()
    line_a = pl.ds(pl.multiple_of(y * 64, 64), 64)
    line_b = pl.ds(pl.multiple_of(256 + x * 64, 64), 64)
    for i in range(3):
        wbig.append(remote(wo.at[far_j, line_a], wo.at[far_j, line_a], S_WB + i, y_peers[i]))
        wbig.append(remote(wo.at[far_j, line_b], wo.at[far_j, line_b], S_WB + 3 + i, x_peers[i]))
    for cp in wbig:
        cp.start()
    for at in xd:
        xd[at].wait_recv()
    project_own(1 - k)
    wd = remote(w_out, wo.at[own_j], S_WD, other)
    wd.start()
    xf[1].wait_recv()
    project_far(1)
    filter_own(k)
    xz[0].wait_recv()
    xf[0].start()
    xf[0].wait_recv()
    project_far(0)
    filter_own(1 - k)
    xz[2].wait_recv()
    xf[2].start()
    xf[2].wait_recv()
    project_far(2)
    filter_early()
    wc = remote(wo.at[far_j], wo.at[far_j], S_WC, other)
    for at in (3, 4):
        xz[at].wait_recv()
        xf[at].start()
    for at in (3, 4):
        xf[at].wait_recv()
    project_far(3)

    m0, m1, m2, sg = 2 * p, 1 - p, 3 - 2 * p, 2 + p
    ez, ex, ey, sends = {}, {}, {}, {}

    def power(g, n):
        return jnp.exp(lam[g] * (-float(ROWS) * jnp.asarray(n).astype(F32)))

    def fall_over(g, tokens):
        return jnp.exp(lam[g] * -float(tokens))

    def send_z(g):
        one = power(g, 1)
        for i in range(2):
            ea[i, g] = et[2 + i, g]
            et[2 + i, g] = fall_over(g, LATE) * et[2 + i, g] + et[4 + i, g]
        mq[g, 0] = (et[m2, g] + one * (et[m1, g] + one * et[m0, g])).astype(STATE)
        mq[g, 1] = et[sg, g].astype(STATE)
        ez[g] = remote(mq.at[g], rz.at[g], S_EZ + g, mirror)
        ez[g].start()

    def send_x(g):
        cm, cq = power(g, 1 - p), power(g, 3 * p)
        ez[g].wait_recv()
        own, far = mq[g].astype(F32), rz[g].astype(F32)
        r1[g, x, h] = (cm * own[0] + cq * far[1]).astype(STATE)
        r1[g, x, 1 - h] = (cm * far[0] + cq * own[1]).astype(STATE)
        ex[g] = [remote(r1.at[g, x], r1.at[g, x], S_EX + 3 * g + i, x_peers[i]) for i in range(3)]
        for cp in ex[g]:
            cp.start()

    def send_y(g):
        group = power(g, 4)
        for cp in ex[g]:
            cp.wait_recv()
        for hh in range(2):
            run = jnp.zeros((MODES, 128), F32)
            pre = run
            for xx in range(4):
                pre = jnp.where(x == xx, run, pre)
                run = group * run + r1[g, xx, hh].astype(F32)
            bf[g, hh] = pre
            r2[g, y, hh] = run.astype(STATE)
        ey[g] = [remote(r2.at[g, y], r2.at[g, y], S_EY + 3 * g + i, y_peers[i]) for i in range(3)]
        for cp in ey[g]:
            cp.start()

    def states(g):
        line = power(g, 16)
        to_x = power(g, 4 * x)
        to_y = power(g, 16 * y)
        one = power(g, 1)
        for cp in ey[g]:
            cp.wait_recv()
        into = []
        plane = None
        for hh in range(2):
            run = jnp.zeros((MODES, 128), F32)
            pre = run
            for yy in range(4):
                pre = jnp.where(y == yy, run, pre)
                run = line * run + r2[g, yy, hh].astype(F32)
            if hh == 1:
                pre = pre + to_y * plane
            plane = run
            into.append(to_x * pre + bf[g, hh])
        mine = jnp.where(h == 0, into[0], into[1])
        theirs = jnp.where(h == 0, into[1], into[0])
        pf = p.astype(F32)
        s_main = power(g, p) * mine + pf * rz[g, 1].astype(F32)
        sin[sg, g] = power(g, 3 * (1 - p)) * theirs + (1.0 - pf) * rz[g, 0].astype(F32)
        sin[m0, g] = s_main
        s_main = one * s_main + et[m0, g]
        sin[m1, g] = s_main
        sin[m2, g] = one * s_main + et[m1, g]
        for i in range(2):
            sin[4 + i, g] = fall_over(g, EARLY) * sin[2 + i, g] + ea[i, g]

    piece = lax.broadcasted_iota(jnp.int32, (1, 8, 128), 1).astype(F32)

    def finish_part(ref, base, steps, unit, g, dst, first):
        base = base + g
        came = jnp.stack([jnp.broadcast_to(sin[unit, g, pl.ds(r, 1), :], (8, 128)) for r in range(MODES)])
        state = wb[g] * (xe[unit * LG + g] + jnp.exp(lb[g] * piece * float(-steps)) * came)

        def body(n, state):
            places = [spread(steps, n * UNROLL + u) for u in range(UNROLL)]
            values = [(ref[base, at, :], ref[base + 8, at, :]) for at in places]
            gated = []
            for q, v in values:
                state = ab[g] * state
                gated.append(q * (v + mode_sum(state)))
            for at, v in zip(places, gated):
                ref[base + 8, at, :] = v
            return state

        lax.fori_loop(0, steps // UNROLL, body, state)
        dst[pl.ds(first, PIECES * steps), :] = ref[base + 8, pl.ds(HALO, PIECES * steps), :].astype(BF)

    def finish(slot, g, dst, far):
        if far:
            finish_part(proj, slot * 12, EARLY // PIECES, slot, g, dst, 0)
            finish_part(late, (slot - 2) * 12, LATE // PIECES, slot + 2, g, dst, EARLY)
        else:
            finish_part(proj, slot * 12, ROWS // PIECES, slot, g, dst, 0)

    def finish_send(i, slot, to, g):
        finish(slot, g, gs.at[i, g], i < 2)
        sends[i, g] = remote(gs.at[i, g], gg.at[own_j, g], S_G + 3 * g + i, to)
        sends[i, g].start()

    def finish_far(g):
        finish_send(0, 2 + k, partner, g)
        finish_send(1, 3 - k, gate_to, g)

    for g in range(LG):
        filter_late(g)
        send_z(g)
    filter_rest(0)
    for g in range(LG):
        send_x(g)
    filter_rest(1)
    for g in range(LG):
        send_y(g)
    for cp in wbig:
        cp.wait_recv()
    wc.start()
    filter_rest(2)
    states(0)
    finish_far(0)
    filter_rest(3)
    for at in xz:
        xz[at].wait_send()
        xd[at].wait_send()
    res_copy = local(tok, xo.at[k, pl.ds(HALO, ROWS)], L_RES)
    res_copy.start()
    for g in range(1, LG):
        states(g)
        finish_far(g)
    for g in range(LG):
        finish_send(2, 1 - k, other, g)
    for g in range(LG):
        finish(k, g, gg.at[own_j, g], False)

    wo_copy.wait()
    res_copy.wait()

    def out_pass(js, halves, kind):
        def body(n, _):
            cols = pl.ds(pl.multiple_of(n * OUT_COLS, OUT_COLS), OUT_COLS)
            tiles = OUT_COLS // 128
            if kind == 0:
                v = xo[k, pl.ds(HALO, ROWS), cols].astype(F32)
            else:
                v = jnp.concatenate([proj[n * tiles + i, pl.ds(0, ROWS), :] for i in range(tiles)], axis=1)
            for j in js:
                for half in halves:
                    lhs = jnp.concatenate([gg[j, 2 * half], gg[j, 2 * half + 1]], axis=1)
                    rows = slice(half * 256, half * 256 + 256)
                    v = v + jnp.dot(lhs, wo[j, rows, cols], preferred_element_type=F32)
            if kind == 2:
                xo[1 - k, pl.ds(0, ROWS), cols] = v.astype(BF)
                local(xo.at[1 - k, pl.ds(0, ROWS), cols], out.at[:, cols], L_OUT + n).start()
            else:
                for i in range(tiles):
                    proj[n * tiles + i, pl.ds(0, ROWS), :] = v[:, i * 128 : (i + 1) * 128]
            return 0

        lax.fori_loop(0, OUT_TILES, body, 0)

    wd.wait_recv()
    for g in range(LG):
        sends[2, g].wait_recv()
    out_pass((own_j, oth_j), (0, 1), 0)
    wc.wait_recv()
    for half in (0, 1):
        for g in (2 * half, 2 * half + 1):
            for i in range(2):
                sends[i, g].wait_recv()
        out_pass((far_j, far2_j), (half,), 1 + half)

    for cp in [halo_copy] + wz + wa + wbig + [wd, wc] + list(xf.values()) + list(ez.values()) + list(sends.values()):
        cp.wait_send()
    for g in range(LG):
        for cp in ex[g] + ey[g]:
            cp.wait_send()
    for n in range(OUT_TILES):
        cols = pl.ds(n * OUT_COLS, OUT_COLS)
        local(xo.at[1 - k, pl.ds(0, ROWS), cols], out.at[:, cols], L_OUT + n).wait()


COPIES = 4


def place(src, out, sems):
    part = ROWS // COPIES
    copies = []
    for i in range(COPIES):
        rows = pl.ds(i * part, part)
        copies.append(pltpu.make_async_copy(src.at[rows], out.at[rows], sems.at[i]))
        copies[-1].start()
    for cp in copies:
        cp.wait()


def shards(tokens, norm_gain, w_in, short_weight, conv_bias, decay_rates, residues, w_out):
    vmem = pl.BlockSpec(memory_space=pltpu.VMEM)
    hbm = pl.BlockSpec(memory_space=pl.ANY)
    mixed = pl.pallas_call(
        kernel,
        out_shape=jax.ShapeDtypeStruct((ROWS, WIDTH), BF),
        in_specs=[hbm, vmem, hbm, vmem, vmem, vmem, vmem, hbm],
        out_specs=hbm,
        scratch_shapes=[
            pltpu.VMEM((2, SLOT, WIDTH), BF),
            pltpu.VMEM((2 * SLOT, WIDTH), BF),
            pltpu.VMEM((3, WIDTH, CH), BF),
            pltpu.VMEM((4, CH, WIDTH), BF),
            pltpu.VMEM((48, SLOT, 128), F32),
            pltpu.VMEM((24, HALO + LATE, 128), F32),
            pltpu.VMEM((3, LG, ROWS, 128), BF),
            pltpu.VMEM((4, LG, ROWS, 128), BF),
            pltpu.VMEM((LG, TAPS, 3, 8, 128), F32),
            pltpu.VMEM((LG, MODES, 8, 128), F32),
            pltpu.VMEM((LG, MODES, 8, 128), F32),
            pltpu.VMEM((LG, MODES, 8, 128), F32),
            pltpu.VMEM((LG, 8, 128), F32),
            pltpu.VMEM((LG, MODES, 128), F32),
            pltpu.VMEM((6 * LG, MODES, 8, 128), F32),
            pltpu.VMEM((6, LG, MODES, 128), F32),
            pltpu.VMEM((2, LG, MODES, 128), F32),
            pltpu.VMEM((6, LG, MODES, 128), F32),
            pltpu.VMEM((1, WIDTH), F32),
            pltpu.VMEM((LG, 2, MODES, 128), F32),
            pltpu.VMEM((LG, 2, MODES, 128), STATE),
            pltpu.VMEM((LG, 2, MODES, 128), STATE),
            pltpu.VMEM((LG, 4, 2, MODES, 128), STATE),
            pltpu.VMEM((LG, 4, 2, MODES, 128), STATE),
            pltpu.SemaphoreType.DMA((S_N,)),
            pltpu.SemaphoreType.DMA((S_N,)),
            pltpu.SemaphoreType.DMA((L_N,)),
        ],
        compiler_params=pltpu.CompilerParams(
            collective_id=0, has_side_effects=True, vmem_limit_bytes=60 * 2**20
        ),
        cost_estimate=pl.CostEstimate(flops=26 * 10**9, bytes_accessed=25 * 2**20, transcendentals=0),
    )(
        tokens,
        norm_gain.reshape(WIDTH // 128, 128),
        w_in.transpose(1, 0, 2),
        short_weight.transpose(1, 0, 2),
        conv_bias.reshape(1, CH),
        decay_rates,
        residues,
        w_out,
    )
    return pl.pallas_call(
        place,
        out_shape=jax.ShapeDtypeStruct((ROWS, WIDTH), BF),
        in_specs=[vmem],
        out_specs=hbm,
        scratch_shapes=[pltpu.SemaphoreType.DMA((COPIES,))],
    )(mixed)


def solution(mesh):
    in_specs = (
        P(("ctx", "tp"), None),
        P(),
        P(None, None, "tp"),
        P(None, None, "tp"),
        P("tp"),
        P(None, "tp"),
        P(None, "tp"),
        P("tp", None),
    )
    return jax.shard_map(
        shards, mesh=mesh, in_specs=in_specs, out_specs=P(("ctx", "tp"), None), check_vma=False
    )
```

```python
import functools

import jax
import jax.numpy as jnp
from jax import lax
from jax.experimental import pallas as pl
from jax.experimental.pallas import tpu as pltpu
from jax.sharding import PartitionSpec as P

MESH = pl.DeviceIdType.MESH
BF, F32 = jnp.bfloat16, jnp.float32
STATE = BF

ROWS = 384
HALO = 16
SLOT = ROWS + HALO
WIDTH = 4096
CH = 512
FIRST = (0, 112, 208, 304)
COUNT = (112, 96, 96, 96)
CHUNKS = 4
ORDER = (1, 0, 2, 3)
PARTS = ((0, 0, 112), (1, 0, 96), (2, 0, 96), (3, 0, 48), (3, 48, 48))
LATE = 96
EARLY = ROWS - LATE
PIECES = 8
MODES = 16
TAPS = 7
LG = CH // 128
UNROLL = 12

S_HALO = 0
S_XZ = 1
S_XD = S_XZ + len(PARTS)
S_XF = S_XD + len(PARTS)
S_WZ = S_XF + len(PARTS)
S_WD = S_WZ + 2
S_WA = S_WD + 1
S_WB = S_WA + 6
S_WC = S_WB + 6
S_EZ = S_WC + 1
S_EX = S_EZ + LG
S_EY = S_EX + 3 * LG
S_G = S_EY + 3 * LG
S_N = S_G + 3 * LG
L_TOK = 0
L_WIN = CHUNKS
L_WO = L_WIN + 3
L_RES = L_WO + 1
L_OUT = L_RES + 1
OUT_TILES = 4
L_N = L_OUT + OUT_TILES
OUT_COLS = WIDTH // OUT_TILES


def kernel(
    tok, gain, w3, taps, bias, decay, resid, w_out, out,
    xo, xr, wi, wo, proj, late, gs, gg, tapb, ab, wb, lb, bb, lam, xe, et, ea, sin, grow, bf, mq, rz, r1, r2, ss, rs, ls,
):
    ctx = lax.axis_index("ctx")
    tp = lax.axis_index("tp")
    x = lax.rem(ctx, 4)
    y = lax.rem(lax.div(ctx, 4), 4)
    h = lax.div(ctx, 16)
    p = lax.div(tp, 2)
    k = lax.rem(tp, 2)
    z = 2 * h + p
    s = 2 * k - 1

    def dev(dx, dy, dz, core):
        zz = lax.rem(dz + 4, 4)
        return (lax.div(zz, 2) * 16 + lax.rem(dy, 4) * 4 + lax.rem(dx, 4), lax.rem(zz, 2) * 2 + core)

    order_at = ctx * 4 + tp
    nxt = lax.rem(order_at + 1, 128)
    prv = lax.rem(order_at + 127, 128)
    nxt = (lax.div(nxt, 4), lax.rem(nxt, 4))
    prv = (lax.div(prv, 4), lax.rem(prv, 4))
    other = dev(x, y, z, 1 - k)
    partner = dev(x, y, z + s, 1 - k)
    gate_to = dev(x, y, z - s, k)
    gate_from = dev(x, y, z + s, k)
    x_peers = [dev(x + d, y, z, k) for d in (1, 2, 3)]
    y_peers = [dev(x, y + d, z, k) for d in (1, 2, 3)]
    mirror = dev(x, y, z + 2, k)
    own_j = 2 * p + k
    oth_j = 2 * p + 1 - k
    far_j = 2 * (1 - p) + 1 - k
    far2_j = 2 * (1 - p) + k

    def remote(src, dst, at, to):
        return pltpu.make_async_remote_copy(
            src_ref=src, dst_ref=dst, send_sem=ss.at[at], recv_sem=rs.at[at], device_id=to, device_id_type=MESH
        )

    def local(src, dst, at):
        return pltpu.make_async_copy(src, dst, ls.at[at])

    tok_copies = {}
    for c in ORDER:
        to = max(FIRST[c], HALO)
        count = FIRST[c] + COUNT[c] - to
        tok_copies[c] = local(tok.at[pl.ds(to - HALO, count)], xo.at[k, pl.ds(to, count)], L_TOK + c)
        tok_copies[c].start()
    win_copies = [local(w3.at[i], wi.at[i], L_WIN + i) for i in range(3)]
    for cp in win_copies:
        cp.start()
    wo_copy = local(w_out, wo.at[own_j], L_WO)

    barrier = pltpu.get_barrier_semaphore()
    greet = [nxt, prv, other, partner, gate_to, gate_from, mirror] + x_peers + y_peers
    for to in greet:
        pl.semaphore_signal(barrier, inc=1, device_id=to, device_id_type=MESH)
    pl.semaphore_wait(barrier, len(greet))

    halo_copy = remote(tok.at[pl.ds(ROWS - HALO, HALO)], xo.at[1 - k, pl.ds(0, HALO)], S_HALO, nxt)
    halo_copy.start()
    row_a = pl.multiple_of((y * 4 + x) * 16, 16)
    row_b = pl.multiple_of(256 + (x * 4 + y) * 16, 16)
    wz = [
        remote(w_out.at[pl.ds(r, 16)], wo.at[own_j, pl.ds(r, 16)], S_WZ + i, partner)
        for i, r in enumerate((row_a, row_b))
    ]
    for cp in wz:
        cp.start()

    for i in range(WIDTH // 128):
        grow[:, i * 128 : (i + 1) * 128] = gain[i : i + 1, :].astype(F32)

    def norm_rows(first, count):
        def body(i, _):
            at = pl.ds(pl.multiple_of(first + i * 16, 16), 16)
            v = xo[k, at, :].astype(F32)
            total = v[:, :128] * v[:, :128]
            for n in range(1, WIDTH // 128):
                total = total + v[:, n * 128 : (n + 1) * 128] * v[:, n * 128 : (n + 1) * 128]
            scale = lax.rsqrt(jnp.sum(total, axis=1, keepdims=True) * (1.0 / WIDTH) + 1e-6)
            xo[k, at, :] = (v * scale * grow[...]).astype(BF)
            return 0

        lax.fori_loop(0, count // 16, body, 0)

    xz, xd, xf = {}, {}, {}
    for c in ORDER:
        tok_copies[c].wait()
        if c == 0:
            halo_copy.wait_recv()

            @pl.when(order_at == 0)
            def _():
                xo[k, pl.ds(0, HALO), :] = jnp.zeros((HALO, WIDTH), BF)

        norm_rows(FIRST[c], COUNT[c])
        for at, (chunk, off, count) in enumerate(PARTS):
            if chunk != c:
                continue

            def landed(core):
                row = 2 * FIRST[c] + core * COUNT[c] + off
                return xr.at[pl.ds(pl.multiple_of(row, 16), count)]

            part = xo.at[k, pl.ds(FIRST[c] + off, count)]
            xz[at] = remote(part, landed(1 - k), S_XZ + at, partner)
            xz[at].start()
            xd[at] = remote(part, part, S_XD + at, other)
            xd[at].start()
            xf[at] = remote(landed(k), landed(k), S_XF + at, other)

    for cp in wz:
        cp.wait_recv()
    wa, wbig = [], []
    for i in range(3):
        wa.append(remote(wo.at[far_j, pl.ds(row_a, 16)], wo.at[far_j, pl.ds(row_a, 16)], S_WA + i, x_peers[i]))
        wa.append(remote(wo.at[far_j, pl.ds(row_b, 16)], wo.at[far_j, pl.ds(row_b, 16)], S_WA + 3 + i, y_peers[i]))
    for cp in wa:
        cp.start()

    rate = decay[...]
    weight = resid[...] * jnp.sqrt(2.0 * rate)
    fall = jnp.exp(-rate)
    tap_rows = taps[...].astype(F32)
    for g in range(LG):
        cols = slice(g * 128, (g + 1) * 128)
        lam[g] = rate[:, cols]
        bb[g] = jnp.broadcast_to(bias[:, cols], (8, 128))
        for r in range(MODES):
            lb[g, r] = jnp.broadcast_to(rate[r : r + 1, cols], (8, 128))
            ab[g, r] = jnp.broadcast_to(fall[r : r + 1, cols], (8, 128))
            wb[g, r] = jnp.broadcast_to(weight[r : r + 1, cols], (8, 128))
        for j in range(TAPS):
            for i in range(3):
                tapb[g, j, i] = jnp.broadcast_to(tap_rows[i, j : j + 1, cols], (8, 128))

    def project_own(slot):
        def body(n, _):
            v = jnp.dot(xo[slot], wi[n], preferred_element_type=F32)
            for b in range(4):
                proj[slot * 12 + 4 * n + b] = v[:, b * 128 : (b + 1) * 128]
            return 0

        lax.fori_loop(0, 3, body, 0, unroll=3)

    def project_far(c):
        first, count = FIRST[c], COUNT[c]

        def body(n, _):
            v = jnp.dot(xr[pl.ds(2 * first, 2 * count)], wi[n], preferred_element_type=F32)
            for a in range(2):
                for b in range(4):
                    part = v[a * count : (a + 1) * count, b * 128 : (b + 1) * 128]
                    if c < CHUNKS - 1:
                        proj[(2 + a) * 12 + 4 * n + b, pl.ds(first, count)] = part
                    else:
                        late[a * 12 + 4 * n + b, pl.ds(HALO, LATE)] = part
                    if c == CHUNKS - 2:
                        late[a * 12 + 4 * n + b, pl.ds(0, HALO)] = part[count - HALO :]
            return 0

        lax.fori_loop(0, 3, body, 0)

    def spread(steps, i):
        return pl.ds(HALO + i, PIECES, stride=steps)

    def fir(ref, base, steps, g, streams):
        base = base + g

        def body(n, past):
            places = [spread(steps, n * UNROLL + u) for u in range(UNROLL)]
            fresh = [[ref[base + 4 * i, at, :] for at in places] for i in streams]
            rows = [list(old) + new for old, new in zip(past, fresh)]
            totals = []
            for i, row in zip(streams, rows):
                stream = []
                for u in range(UNROLL):
                    t = [tapb[g, j, i] * row[u + TAPS - 1 - j] for j in range(TAPS)]
                    stream.append(((t[0] + t[1]) + (t[2] + t[3])) + ((t[4] + t[5]) + t[6]))
                totals.append(stream)
            for u, at in enumerate(places):
                if streams == (0,):
                    ref[base, at, :] = totals[0][u]
                else:
                    ref[base + 4, at, :] = totals[0][u] * totals[1][u]
            return tuple(tuple(row[UNROLL:]) for row in rows)

        past = tuple(
            tuple(ref[base + 4 * i, spread(steps, m - (TAPS - 1)), :] for m in range(TAPS - 1)) for i in streams
        )
        lax.fori_loop(0, steps // UNROLL, body, past)

    lane8 = lax.broadcasted_iota(jnp.int32, (1, 8, 128), 1)

    def mode_sum(v):
        count = MODES
        while count > 1:
            count //= 2
            v = v[:count] + v[count:]
        return v[0]

    def scan(ref, base, steps, unit, g, outputs, ends):
        base = base + g

        def body(n, state):
            places = [spread(steps, n * UNROLL + u) for u in range(UNROLL)]
            values = [ref[base + 4, at, :] for at in places]
            sums = []
            for v in values:
                state = ab[g] * state + v[None]
                if outputs:
                    sums.append(mode_sum(wb[g] * state) + bb[g] * v)
            for at, v in zip(places, sums):
                ref[base + 8, at, :] = v
            return state

        v = lax.fori_loop(0, steps // UNROLL, body, jnp.zeros((MODES, 8, 128), F32))
        if not ends:
            return
        step = jnp.exp(lb[g] * float(-steps))
        for d in (1, 2, 4):
            back = pltpu.roll(v, d, 1)
            v = v + jnp.where(lane8 >= d, step * back, 0.0)
            step = step * step
        xe[unit * LG + g] = jnp.where(lane8 >= 1, pltpu.roll(v, 1, 1), 0.0)
        for r in range(MODES):
            et[unit, g, pl.ds(r, 1), :] = v[r, 7:8, :]

    def filter_own(slot):
        def body(g, _):
            fir(proj, slot * 12, ROWS // PIECES, g, (1, 2))
            scan(proj, slot * 12, ROWS // PIECES, slot, g, True, True)
            fir(proj, slot * 12, ROWS // PIECES, g, (0,))
            return 0

        lax.fori_loop(0, LG, body, 0)

    def filter_early():
        def body(n, _):
            i, g = lax.div(n, LG), lax.rem(n, LG)
            fir(proj, 24 + i * 12, EARLY // PIECES, g, (1, 2))
            scan(proj, 24 + i * 12, EARLY // PIECES, 2 + i, g, False, True)
            return 0

        lax.fori_loop(0, 2 * LG, body, 0)

    def filter_late(g):
        for i in range(2):
            fir(late, i * 12, LATE // PIECES, g, (1, 2))
            scan(late, i * 12, LATE // PIECES, 4 + i, g, False, True)

    def filter_rest(g):
        def body(i, _):
            fir(proj, 24 + i * 12, EARLY // PIECES, g, (0,))
            scan(proj, 24 + i * 12, EARLY // PIECES, 0, g, True, False)
            fir(late, i * 12, LATE // PIECES, g, (0,))
            scan(late, i * 12, LATE // PIECES, 0, g, True, False)
            return 0

        lax.fori_loop(0, 2, body, 0)

    for cp in win_copies:
        cp.wait()
    wo_copy.start()
    project_own(k)
    xz[1].wait_recv()
    xf[1].start()
    wbig = []
    for cp in wa:
        cp.wait_recv()
    line_a = pl.ds(pl.multiple_of(y * 64, 64), 64)
    line_b = pl.ds(pl.multiple_of(256 + x * 64, 64), 64)
    for i in range(3):
        wbig.append(remote(wo.at[far_j, line_a], wo.at[far_j, line_a], S_WB + i, y_peers[i]))
        wbig.append(remote(wo.at[far_j, line_b], wo.at[far_j, line_b], S_WB + 3 + i, x_peers[i]))
    for cp in wbig:
        cp.start()
    for at in xd:
        xd[at].wait_recv()
    project_own(1 - k)
    wd = remote(w_out, wo.at[own_j], S_WD, other)
    wd.start()
    xf[1].wait_recv()
    project_far(1)
    filter_own(k)
    xz[0].wait_recv()
    xf[0].start()
    xf[0].wait_recv()
    project_far(0)
    filter_own(1 - k)
    xz[2].wait_recv()
    xf[2].start()
    xf[2].wait_recv()
    project_far(2)
    filter_early()
    wc = remote(wo.at[far_j], wo.at[far_j], S_WC, other)
    for at in (3, 4):
        xz[at].wait_recv()
        xf[at].start()
    for at in (3, 4):
        xf[at].wait_recv()
    project_far(3)

    m0, m1, m2, sg = 2 * p, 1 - p, 3 - 2 * p, 2 + p
    ez, ex, ey, sends = {}, {}, {}, {}

    def power(g, n):
        return jnp.exp(lam[g] * (-float(ROWS) * jnp.asarray(n).astype(F32)))

    def fall_over(g, tokens):
        return jnp.exp(lam[g] * -float(tokens))

    def send_z(g):
        one = power(g, 1)
        for i in range(2):
            ea[i, g] = et[2 + i, g]
            et[2 + i, g] = fall_over(g, LATE) * et[2 + i, g] + et[4 + i, g]
        mq[g, 0] = (et[m2, g] + one * (et[m1, g] + one * et[m0, g])).astype(STATE)
        mq[g, 1] = et[sg, g].astype(STATE)
        ez[g] = remote(mq.at[g], rz.at[g], S_EZ + g, mirror)
        ez[g].start()

    def send_x(g):
        cm, cq = power(g, 1 - p), power(g, 3 * p)
        ez[g].wait_recv()
        own, far = mq[g].astype(F32), rz[g].astype(F32)
        r1[g, x, h] = (cm * own[0] + cq * far[1]).astype(STATE)
        r1[g, x, 1 - h] = (cm * far[0] + cq * own[1]).astype(STATE)
        ex[g] = [remote(r1.at[g, x], r1.at[g, x], S_EX + 3 * g + i, x_peers[i]) for i in range(3)]
        for cp in ex[g]:
            cp.start()

    def send_y(g):
        group = power(g, 4)
        for cp in ex[g]:
            cp.wait_recv()
        for hh in range(2):
            run = jnp.zeros((MODES, 128), F32)
            pre = run
            for xx in range(4):
                pre = jnp.where(x == xx, run, pre)
                run = group * run + r1[g, xx, hh].astype(F32)
            bf[g, hh] = pre
            r2[g, y, hh] = run.astype(STATE)
        ey[g] = [remote(r2.at[g, y], r2.at[g, y], S_EY + 3 * g + i, y_peers[i]) for i in range(3)]
        for cp in ey[g]:
            cp.start()

    def states(g):
        line = power(g, 16)
        to_x = power(g, 4 * x)
        to_y = power(g, 16 * y)
        one = power(g, 1)
        for cp in ey[g]:
            cp.wait_recv()
        into = []
        plane = None
        for hh in range(2):
            run = jnp.zeros((MODES, 128), F32)
            pre = run
            for yy in range(4):
                pre = jnp.where(y == yy, run, pre)
                run = line * run + r2[g, yy, hh].astype(F32)
            if hh == 1:
                pre = pre + to_y * plane
            plane = run
            into.append(to_x * pre + bf[g, hh])
        mine = jnp.where(h == 0, into[0], into[1])
        theirs = jnp.where(h == 0, into[1], into[0])
        pf = p.astype(F32)
        s_main = power(g, p) * mine + pf * rz[g, 1].astype(F32)
        sin[sg, g] = power(g, 3 * (1 - p)) * theirs + (1.0 - pf) * rz[g, 0].astype(F32)
        sin[m0, g] = s_main
        s_main = one * s_main + et[m0, g]
        sin[m1, g] = s_main
        sin[m2, g] = one * s_main + et[m1, g]
        for i in range(2):
            sin[4 + i, g] = fall_over(g, EARLY) * sin[2 + i, g] + ea[i, g]

    piece = lax.broadcasted_iota(jnp.int32, (1, 8, 128), 1).astype(F32)

    def finish_part(ref, base, steps, unit, g, dst, first):
        base = base + g
        came = jnp.stack([jnp.broadcast_to(sin[unit, g, pl.ds(r, 1), :], (8, 128)) for r in range(MODES)])
        state = wb[g] * (xe[unit * LG + g] + jnp.exp(lb[g] * piece * float(-steps)) * came)

        def body(n, state):
            places = [spread(steps, n * UNROLL + u) for u in range(UNROLL)]
            values = [(ref[base, at, :], ref[base + 8, at, :]) for at in places]
            gated = []
            for q, v in values:
                state = ab[g] * state
                gated.append(q * (v + mode_sum(state)))
            for at, v in zip(places, gated):
                ref[base + 8, at, :] = v
            return state

        lax.fori_loop(0, steps // UNROLL, body, state)
        dst[pl.ds(first, PIECES * steps), :] = ref[base + 8, pl.ds(HALO, PIECES * steps), :].astype(BF)

    def finish(slot, g, dst, far):
        if far:
            finish_part(proj, slot * 12, EARLY // PIECES, slot, g, dst, 0)
            finish_part(late, (slot - 2) * 12, LATE // PIECES, slot + 2, g, dst, EARLY)
        else:
            finish_part(proj, slot * 12, ROWS // PIECES, slot, g, dst, 0)

    def finish_send(i, slot, to, g):
        finish(slot, g, gs.at[i, g], i < 2)
        sends[i, g] = remote(gs.at[i, g], gg.at[own_j, g], S_G + 3 * g + i, to)
        sends[i, g].start()

    def finish_far(g):
        finish_send(0, 2 + k, partner, g)
        finish_send(1, 3 - k, gate_to, g)

    for g in range(LG):
        filter_late(g)
        send_z(g)
    filter_rest(0)
    for g in range(LG):
        send_x(g)
    filter_rest(1)
    for g in range(LG):
        send_y(g)
    for cp in wbig:
        cp.wait_recv()
    wc.start()
    filter_rest(2)
    states(0)
    finish_far(0)
    filter_rest(3)
    for at in xz:
        xz[at].wait_send()
        xd[at].wait_send()
    res_copy = local(tok, xo.at[k, pl.ds(HALO, ROWS)], L_RES)
    res_copy.start()
    for g in range(1, LG):
        states(g)
        finish_far(g)
    for g in range(LG):
        finish_send(2, 1 - k, other, g)
    for g in range(LG):
        finish(k, g, gg.at[own_j, g], False)

    wo_copy.wait()
    res_copy.wait()

    def out_pass(js, halves, kind):
        def body(n, _):
            cols = pl.ds(pl.multiple_of(n * OUT_COLS, OUT_COLS), OUT_COLS)
            tiles = OUT_COLS // 128
            if kind == 0:
                v = xo[k, pl.ds(HALO, ROWS), cols].astype(F32)
            else:
                v = jnp.concatenate([proj[n * tiles + i, pl.ds(0, ROWS), :] for i in range(tiles)], axis=1)
            for j in js:
                for half in halves:
                    lhs = jnp.concatenate([gg[j, 2 * half], gg[j, 2 * half + 1]], axis=1)
                    rows = slice(half * 256, half * 256 + 256)
                    v = v + jnp.dot(lhs, wo[j, rows, cols], preferred_element_type=F32)
            if kind == 2:
                xo[1 - k, pl.ds(0, ROWS), cols] = v.astype(BF)
                local(xo.at[1 - k, pl.ds(0, ROWS), cols], out.at[:, cols], L_OUT + n).start()
            else:
                for i in range(tiles):
                    proj[n * tiles + i, pl.ds(0, ROWS), :] = v[:, i * 128 : (i + 1) * 128]
            return 0

        lax.fori_loop(0, OUT_TILES, body, 0)

    wd.wait_recv()
    for g in range(LG):
        sends[2, g].wait_recv()
    out_pass((own_j, oth_j), (0, 1), 0)
    wc.wait_recv()
    for half in (0, 1):
        for g in (2 * half, 2 * half + 1):
            for i in range(2):
                sends[i, g].wait_recv()
        out_pass((far_j, far2_j), (half,), 1 + half)

    for cp in [halo_copy] + wz + wa + wbig + [wd, wc] + list(xf.values()) + list(ez.values()) + list(sends.values()):
        cp.wait_send()
    for g in range(LG):
        for cp in ex[g] + ey[g]:
            cp.wait_send()
    for n in range(OUT_TILES):
        cols = pl.ds(n * OUT_COLS, OUT_COLS)
        local(xo.at[1 - k, pl.ds(0, ROWS), cols], out.at[:, cols], L_OUT + n).wait()


COPIES = 8


def place(src, out, held, first, second):
    part = ROWS // COPIES
    loads, stores = [], []
    for i in range(COPIES):
        rows = pl.ds(i * part, part)
        loads.append(pltpu.make_async_copy(src.at[rows], held.at[rows], first.at[i]))
        stores.append(pltpu.make_async_copy(held.at[rows], out.at[rows], second.at[i]))
        loads[-1].start()
    for load, store in zip(loads, stores):
        load.wait()
        store.start()
    for store in stores:
        store.wait()


def shards(tokens, norm_gain, w_in, short_weight, conv_bias, decay_rates, residues, w_out):
    vmem = pl.BlockSpec(memory_space=pltpu.VMEM)
    hbm = pl.BlockSpec(memory_space=pl.ANY)
    mixed = pl.pallas_call(
        kernel,
        out_shape=jax.ShapeDtypeStruct((ROWS, WIDTH), BF),
        in_specs=[hbm, vmem, hbm, vmem, vmem, vmem, vmem, hbm],
        out_specs=hbm,
        scratch_shapes=[
            pltpu.VMEM((2, SLOT, WIDTH), BF),
            pltpu.VMEM((2 * SLOT, WIDTH), BF),
            pltpu.VMEM((3, WIDTH, CH), BF),
            pltpu.VMEM((4, CH, WIDTH), BF),
            pltpu.VMEM((48, SLOT, 128), F32),
            pltpu.VMEM((24, HALO + LATE, 128), F32),
            pltpu.VMEM((3, LG, ROWS, 128), BF),
            pltpu.VMEM((4, LG, ROWS, 128), BF),
            pltpu.VMEM((LG, TAPS, 3, 8, 128), F32),
            pltpu.VMEM((LG, MODES, 8, 128), F32),
            pltpu.VMEM((LG, MODES, 8, 128), F32),
            pltpu.VMEM((LG, MODES, 8, 128), F32),
            pltpu.VMEM((LG, 8, 128), F32),
            pltpu.VMEM((LG, MODES, 128), F32),
            pltpu.VMEM((6 * LG, MODES, 8, 128), F32),
            pltpu.VMEM((6, LG, MODES, 128), F32),
            pltpu.VMEM((2, LG, MODES, 128), F32),
            pltpu.VMEM((6, LG, MODES, 128), F32),
            pltpu.VMEM((1, WIDTH), F32),
            pltpu.VMEM((LG, 2, MODES, 128), F32),
            pltpu.VMEM((LG, 2, MODES, 128), STATE),
            pltpu.VMEM((LG, 2, MODES, 128), STATE),
            pltpu.VMEM((LG, 4, 2, MODES, 128), STATE),
            pltpu.VMEM((LG, 4, 2, MODES, 128), STATE),
            pltpu.SemaphoreType.DMA((S_N,)),
            pltpu.SemaphoreType.DMA((S_N,)),
            pltpu.SemaphoreType.DMA((L_N,)),
        ],
        compiler_params=pltpu.CompilerParams(
            collective_id=0, has_side_effects=True, vmem_limit_bytes=60 * 2**20
        ),
        cost_estimate=pl.CostEstimate(flops=26 * 10**9, bytes_accessed=25 * 2**20, transcendentals=0),
    )(
        tokens,
        norm_gain.reshape(WIDTH // 128, 128),
        w_in.transpose(1, 0, 2),
        short_weight.transpose(1, 0, 2),
        conv_bias.reshape(1, CH),
        decay_rates,
        residues,
        w_out,
    )
    return pl.pallas_call(
        place,
        out_shape=jax.ShapeDtypeStruct((ROWS, WIDTH), BF),
        in_specs=[hbm],
        out_specs=hbm,
        scratch_shapes=[
            pltpu.VMEM((ROWS, WIDTH), BF),
            pltpu.SemaphoreType.DMA((COPIES,)),
            pltpu.SemaphoreType.DMA((COPIES,)),
        ],
    )(mixed)


def solution(mesh):
    in_specs = (
        P(("ctx", "tp"), None),
        P(),
        P(None, None, "tp"),
        P(None, None, "tp"),
        P("tp"),
        P(None, "tp"),
        P(None, "tp"),
        P("tp", None),
    )
    return jax.shard_map(
        shards, mesh=mesh, in_specs=in_specs, out_specs=P(("ctx", "tp"), None), check_vma=False
    )
```
